256 devices in a mesh: ea: 128 (over y, z, x), ta: 2 (over core).
Axes of the slice: x: 4, y: 4, z: 8, core: 2. Of those that a mesh axis runs over, the one named last changes fastest.
Arguments:
- sample_inphase: float32 [128, 256, 256], P('ea'), may hold values from 0.2 to 1.2
- sample_quadrature: float32 [128, 256, 256], P('ea'), may hold values from -3 to 3
- beam_inphase: float32 [128, 3, 32, 32], P('ea'), may hold values from -3 to 3
- beam_quadrature: float32 [128, 3, 32, 32], P('ea'), may hold values from -3 to 3
- recorded_diffraction: float32 [128, 2, 16, 32, 32], P('ea', 'ta'), may hold values from 0.05 to 4
- window_corners: int32 [128, 2, 16, 2], P('ea', 'ta'), may hold values from 0 to 224
- filled_tallies: int32 [128, 2], P('ea', 'ta'), may hold values from 1 to 16, 24 in all within a row
- absorption_templates: float32 [16, 128], replicated, may hold values from -6 to 6
Outputs:
- fitted: float32 [2, 128, 128, 2, 256], P(None, 'ea', None, 'ta')
- coefficients: float32 [2, 16, 65536], P(None, None, ('ea', 'ta'))
The draws below stay inside these ranges and needn't reach their ends.
Inputs may be any that keep to these rules, and one draw needn't show every extreme that they name: `filled_tallies`: in each energy the two tiles' counts sum to 24 and the larger is at most 16. `window_corners`: offsets of slots at or past their tile's count are not used.
All inputs are finite; a program needn't handle non-finite values. No bound on the sum of `filled_tallies` on one device may be relied on, other than what follows from the above.
Results may differ from the reference program's by a relative error of at most 0.0003.
Values sent between devices are 32-bit elements; how exact they have to be, the bound alone decides.
A program may use at most 64 MiB of HBM per device.

```python
import math
import jax
import jax.numpy as jnp
import numpy as np
from jax import lax

OBJ = 256
WINDOW_SPAN = 32
MODES = 3
EDGES = 16
BEAM_QUANTA = 128
RASTER_SPOTS = 16
PIX = 256
N_EA = 128
N_TA = 2


def place_ends(result, stream_key, low, largest):
    longest = result.shape.index(max(result.shape))
    spots = []
    for shift in (0, 1):
        where = [jax.random.randint(jax.random.fold_in(stream_key, axis), (), 0, length) for axis, length in enumerate(result.shape)]
        where[longest] = (where[longest] + shift) % result.shape[longest]
        spots.append(tuple(where))
    return result.at[spots[0]].set(low).at[spots[1]].set(largest)


def shard_levels(key, shape, split, smallest, largest):
    level = 1.0
    for dim, shards_of in split:
        heights = jax.random.uniform(jax.random.fold_in(jax.random.fold_in(key, 6), dim), (shards_of,), jnp.float32, smallest / len(split), largest / len(split))
        level = level * jnp.repeat(jnp.exp(heights), shape[dim] // shards_of).reshape((-1,) + (1,) * (len(shape) - 1 - dim))
    return level


def length_profile(amount, total, limit, skew):
    loads = [(1 << 20) // math.isqrt(grade ** skew) + 1 for grade in range(2, amount + 1)]
    spare, counts = total - limit - (amount - 1), [1] * (amount - 1)
    while spare > 0:
        movable = [i for i in range(amount - 1) if counts[i] < limit]
        whole, budget = sum([loads[i] for i in movable]), spare
        for i in movable:
            addition = min(limit - counts[i], max(1, budget * loads[i] // whole), spare)
            counts[i] = counts[i] + addition
            spare = spare - addition
    return np.array([limit] + counts)


def uneven_parts(own_key, number_of, total, bound, skew):
    if number_of == 2:
        one = jax.random.randint(own_key, (), max(1, total - bound), min(bound, total - 1) + 1)
        return jnp.stack([one, total - one])
    sizes = jnp.asarray(length_profile(number_of, total, bound, skew), jnp.int32)
    pairs = (number_of - 1) // 2
    donor, sink = sizes[1:1 + 2 * pairs:2], sizes[2:2 + 2 * pairs:2]
    margin = jnp.minimum(donor - 1, bound - sink)
    moved = jax.random.randint(jax.random.fold_in(own_key, 1), (pairs,), 0, 1 << 20) % (margin + 1)
    sizes = sizes.at[1:1 + 2 * pairs:2].set(donor - moved).at[2:2 + 2 * pairs:2].set(sink + moved)
    return sizes[jax.random.permutation(jax.random.fold_in(own_key, 2), number_of)]


def scatter_about(own_key, shape, scale, limit, cuts=(), kind=jnp.bfloat16):
    result = jax.random.normal(own_key, shape, jnp.float32) * scale
    if len(cuts) > 0:
        result = shard_levels(own_key, shape, cuts, -0.22, 0.18) * result
    return jnp.clip(result, min=-limit, max=limit).astype(kind)


def setup_inputs(seed: int = 0) -> dict:
    key_list = jax.random.split(jax.random.key(seed), 9)
    return {
        "sample_inphase": jnp.clip(0.2 + 1 * jax.random.uniform(key_list[0], (BEAM_QUANTA, OBJ, OBJ), jnp.float32) ** shard_levels(key_list[0], (BEAM_QUANTA, OBJ, OBJ), ((0, 128),), -0.2, 0.2), 0.2, 1.2),
        "sample_quadrature": scatter_about(key_list[1], (BEAM_QUANTA, OBJ, OBJ), 0.5, 3.0, ((0, 128),), jnp.float32),
        "beam_inphase": scatter_about(key_list[2], (BEAM_QUANTA, MODES, WINDOW_SPAN, WINDOW_SPAN), 0.5, 3.0, ((0, 128),), jnp.float32),
        "beam_quadrature": scatter_about(key_list[3], (BEAM_QUANTA, MODES, WINDOW_SPAN, WINDOW_SPAN), 0.5, 3.0, ((0, 128),), jnp.float32),
        "recorded_diffraction": jnp.clip(jnp.exp(math.log(4.0) - 4.3820266 * jax.random.uniform(key_list[4], (BEAM_QUANTA, N_TA, RASTER_SPOTS, WINDOW_SPAN, WINDOW_SPAN), jnp.float32) ** shard_levels(key_list[4], (BEAM_QUANTA, N_TA, RASTER_SPOTS, WINDOW_SPAN, WINDOW_SPAN), ((0, 128), (1, 2)), -0.2, 0.2)), 0.05, 4.0),
        "window_corners": place_ends(jax.random.randint(key_list[5], (BEAM_QUANTA, N_TA, RASTER_SPOTS, 2), 0, OBJ - WINDOW_SPAN + 1), jax.random.fold_in(key_list[5], 1), 0, OBJ - WINDOW_SPAN).astype(jnp.int32),
        "filled_tallies": jax.vmap(lambda own: uneven_parts(own, N_TA, RASTER_SPOTS * 3 // 2, RASTER_SPOTS, 0))(jax.random.split(key_list[6], BEAM_QUANTA)).reshape((BEAM_QUANTA, N_TA)).astype(jnp.int32),
        "absorption_templates": scatter_about(key_list[7], (EDGES, BEAM_QUANTA), 1.0, 6.0, (), jnp.float32),
    }


HIGHEST_PRECISION = lax.Precision.HIGHEST
FLOOR_POWER = 0.5
REGULARIZER = 1.0

def dft_tables(length):
    counter = jnp.arange(length, dtype=jnp.int32)
    product = counter[:, None] * counter[None, :] % length
    angles = 2.0 * jnp.pi / length * product.astype(jnp.float32)
    norming = 1.0 / jnp.sqrt(jnp.float32(length))
    return (jnp.cos(angles) * norming, -jnp.sin(angles) * norming)

def two_sided(field_re, field_im, table_re, table_im):
    left_re = jnp.einsum('jk,...kl->...jl', table_re, field_re, precision=HIGHEST_PRECISION) - jnp.einsum('jk,...kl->...jl', table_im, field_im, precision=HIGHEST_PRECISION)
    left_im = jnp.einsum('jk,...kl->...jl', table_re, field_im, precision=HIGHEST_PRECISION) + jnp.einsum('jk,...kl->...jl', table_im, field_re, precision=HIGHEST_PRECISION)
    right_re = jnp.einsum('...jk,kl->...jl', left_re, table_re, precision=HIGHEST_PRECISION) - jnp.einsum('...jk,kl->...jl', left_im, table_im, precision=HIGHEST_PRECISION)
    right_im = jnp.einsum('...jk,kl->...jl', left_re, table_im, precision=HIGHEST_PRECISION) + jnp.einsum('...jk,kl->...jl', left_im, table_re, precision=HIGHEST_PRECISION)
    return (right_re, right_im)

def slot_terms(sample_inphase, sample_quadrature, beam_inphase, beam_quadrature, intensity, corners, weight, table_re, table_im):
    width = beam_inphase.shape[-1]

    def extract(source, corner):
        return lax.dynamic_slice(source, (corner[0], corner[1]), (width, width))
    patch_re = jax.vmap(extract, (None, 0))(sample_inphase, corners)
    patch_im = jax.vmap(extract, (None, 0))(sample_quadrature, corners)
    exit_re = beam_inphase[None] * patch_re[:, None] - beam_quadrature[None] * patch_im[:, None]
    exit_im = beam_inphase[None] * patch_im[:, None] + beam_quadrature[None] * patch_re[:, None]
    far_re, far_im = two_sided(exit_re, exit_im, table_re, table_im)
    power = lax.optimization_barrier(jnp.sum(far_re * far_re + far_im * far_im, axis=1))
    factor = (1.0 - jnp.sqrt(intensity) / jnp.sqrt(jnp.maximum(power, FLOOR_POWER))) * weight[:, None, None]
    back_re, back_im = two_sided(far_re * factor[:, None], far_im * factor[:, None], table_re, -table_im)
    terms_re = lax.optimization_barrier(jnp.sum(beam_inphase[None] * back_re + beam_quadrature[None] * back_im, axis=1))
    terms_im = lax.optimization_barrier(jnp.sum(beam_inphase[None] * back_im - beam_quadrature[None] * back_re, axis=1))
    return (terms_re, terms_im)

def deposit(field, patch, corner):
    width = patch.shape[0]
    current = lax.dynamic_slice(field, (corner[0], corner[1]), (width, width))
    return lax.dynamic_update_slice(field, current + patch, (corner[0], corner[1]))

def reference(sample_inphase, sample_quadrature, beam_inphase, beam_quadrature, recorded_diffraction, window_corners, filled_tallies, absorption_templates):
    table_re, table_im = dft_tables(WINDOW_SPAN)

    def lone_wavelength(items):
        o_re, o_im, p_re, p_im, intensity_all, corner_all, tile_counts = items
        live = jnp.arange(RASTER_SPOTS, dtype=jnp.int32)[None, :] < tile_counts[:, None]
        weight = live.astype(jnp.float32).reshape(-1)
        intensity = intensity_all.reshape(N_TA * RASTER_SPOTS, WINDOW_SPAN, WINDOW_SPAN)
        corners = corner_all.reshape(N_TA * RASTER_SPOTS, 2)
        terms_re, terms_im = slot_terms(o_re, o_im, p_re, p_im, intensity, corners, weight, table_re, table_im)
        light_patch = lax.optimization_barrier(jnp.sum(p_re * p_re + p_im * p_im, axis=0))

        def add_one(index, carry):
            grad_re, grad_im, light = carry
            corner = corners[index]
            return (deposit(grad_re, terms_re[index], corner), deposit(grad_im, terms_im[index], corner), deposit(light, light_patch * weight[index], corner))
        zeros = jnp.zeros((OBJ, OBJ), jnp.float32)
        grad_re, grad_im, light = lax.fori_loop(0, N_TA * RASTER_SPOTS, add_one, (zeros, zeros, zeros))
        return (o_re - grad_re / (light + REGULARIZER), o_im - grad_im / (light + REGULARIZER))
    revised_inphase, revised_quadrature = lax.map(lone_wavelength, (sample_inphase, sample_quadrature, beam_inphase, beam_quadrature, recorded_diffraction, window_corners, filled_tallies))
    spectra = jnp.stack([revised_inphase.reshape(BEAM_QUANTA, OBJ * OBJ), revised_quadrature.reshape(BEAM_QUANTA, OBJ * OBJ)])
    gram = jnp.dot(absorption_templates, absorption_templates.T, precision=HIGHEST_PRECISION)
    project = jnp.linalg.solve(gram, absorption_templates)
    coefficients = jnp.einsum('ke,cep->ckp', project, spectra, precision=HIGHEST_PRECISION)
    fitted = jnp.einsum('ke,ckp->cep', absorption_templates, coefficients, precision=HIGHEST_PRECISION)
    return (fitted.reshape(2, BEAM_QUANTA, N_EA, N_TA, PIX), coefficients)
```

```python
import functools

import jax
import jax.numpy as jnp
import numpy as np
from jax import lax
from jax.experimental import pallas as pl
from jax.experimental.pallas import tpu as pltpu
from jax.sharding import PartitionSpec as P

MESH = pl.DeviceIdType.MESH
HIGHEST = lax.Precision.HIGHEST
FLOOR_POWER = 0.5
REGULARIZER = 1.0
ENERGIES = 128
EDGES = 16
SIDE = 256
HALF = 128
WIDTH = 32
MODES = 3
SLOTS = 16
PER_GROUP = 4
GROUPS = SLOTS // PER_GROUP
BAND = MODES * WIDTH
LANES = PER_GROUP * WIDTH
VMEM_BYTES = 48 * 1024 * 1024


def split_table(table):
    high = table.astype(jnp.bfloat16)
    low = (table - high.astype(np.float32)).astype(jnp.bfloat16)
    return np.stack([high, low])


def dft_matrices():
    index = np.arange(WIDTH)
    angles = 2.0 * np.pi / WIDTH * (index[:, None] * index[None, :] % WIDTH)
    re, im = np.cos(angles) / np.sqrt(WIDTH), -np.sin(angles) / np.sqrt(WIDTH)
    tables = []
    for sign in (1.0, -1.0):
        b_re, b_im = (np.kron(np.eye(PER_GROUP), part) for part in (re, sign * im))
        l_re, l_im = (np.kron(np.eye(MODES), part) for part in (re, sign * im))
        right = np.block([[b_re, b_im], [-b_im, b_re]]).astype(np.float32)
        left = np.block([[l_re, -l_im], [l_im, l_re]]).astype(np.float32)
        tables += [split_table(right), split_table(left)]
    return tables


def halves(value):
    high = value.astype(jnp.bfloat16)
    return high, (value - high.astype(jnp.float32)).astype(jnp.bfloat16)


def product(a, b):
    dot = functools.partial(jnp.dot, preferred_element_type=jnp.float32)
    return dot(a[0], b[0]) + (dot(a[0], b[1]) + dot(a[1], b[0]))


def slots_kernel(
    corners,
    tallies,
    o_re,
    o_im,
    p_re,
    p_im,
    intensity,
    right_f,
    left_f,
    right_b,
    left_b,
    out,
    objects,
    totals,
):
    tally = tallies[0, 0]
    for part, source in enumerate((o_re, o_im)):
        for half in range(2):
            lanes = slice(half * HALF, (half + 1) * HALF)
            objects[pl.ds(2 * part + half, SIDE, stride=4), :] = source[0, :, lanes]
    totals[...] = jnp.zeros_like(totals)
    probe_re = [jnp.concatenate([p_re[0, m]] * PER_GROUP, axis=1) for m in range(MODES)]
    probe_im = [jnp.concatenate([p_im[0, m]] * PER_GROUP, axis=1) for m in range(MODES)]
    light = sum(a * a + b * b for a, b in zip(probe_re, probe_im))
    lane = lax.broadcasted_iota(jnp.int32, (WIDTH, LANES), 1)

    bands = []
    for g in range(GROUPS):
        patch = [jnp.zeros((WIDTH, LANES), jnp.float32)] * 2
        for j in range(PER_GROUP):
            s = g * PER_GROUP + j
            row, column = corners[s, 0], corners[s, 1]
            shift = lax.rem(WIDTH * j + SIDE - column, HALF)
            for part in range(2):
                left, right = (objects[pl.ds(4 * row + 2 * part + half, WIDTH, stride=4), :] for half in range(2))
                rolled = pltpu.roll(jnp.where(lane >= column, left, right), shift, 1)
                patch[part] = jnp.where(lane // WIDTH == j, rolled, patch[part])
        exits_re = [a * patch[0] - b * patch[1] for a, b in zip(probe_re, probe_im)]
        exits_im = [a * patch[1] + b * patch[0] for a, b in zip(probe_re, probe_im)]
        bands.append(
            jnp.concatenate(
                [jnp.concatenate(exits_re, axis=0), jnp.concatenate(exits_im, axis=0)], axis=1
            )
        )
    wide = product(halves(jnp.concatenate(bands, axis=0)), (right_f[0], right_f[1]))
    tall = jnp.concatenate(
        [
            jnp.concatenate([wide[g * BAND : (g + 1) * BAND, h * LANES : (h + 1) * LANES] for g in range(GROUPS)], axis=1)
            for h in range(2)
        ],
        axis=0,
    )
    far = product((left_f[0], left_f[1]), halves(tall))
    power = sum(
        far[k * WIDTH : (k + 1) * WIDTH] * far[k * WIDTH : (k + 1) * WIDTH] for k in range(2 * MODES)
    )
    measured = jnp.concatenate([intensity[0, 0, s] for s in range(SLOTS)], axis=1)
    used = lax.broadcasted_iota(jnp.int32, (WIDTH, GROUPS * LANES), 1) // WIDTH < tally
    factor = jnp.where(used, 1.0 - jnp.sqrt(measured) / jnp.sqrt(jnp.maximum(power, FLOOR_POWER)), 0.0)
    corrected = far * jnp.concatenate([factor] * (2 * MODES), axis=0)
    tall = product((left_b[0], left_b[1]), halves(corrected))
    wide = jnp.concatenate(
        [
            jnp.concatenate([tall[h * BAND : (h + 1) * BAND, g * LANES : (g + 1) * LANES] for h in range(2)], axis=1)
            for g in range(GROUPS)
        ],
        axis=0,
    )
    back = product(halves(wide), (right_b[0], right_b[1]))
    for g in range(GROUPS):
        term_re, term_im = jnp.zeros((2, WIDTH, LANES), jnp.float32)
        for m in range(MODES):
            rows = slice(g * BAND + m * WIDTH, g * BAND + (m + 1) * WIDTH)
            b_re, b_im = back[rows, :LANES], back[rows, LANES:]
            term_re += probe_re[m] * b_re + probe_im[m] * b_im
            term_im += probe_re[m] * b_im - probe_im[m] * b_re
        for j in range(PER_GROUP):
            s = g * PER_GROUP + j
            row, column = corners[s, 0], corners[s, 1]
            shift = lax.rem(column + HALF - WIDTH * j, HALF)
            weight = jnp.where(s < tally, 1.0, 0.0)
            for field, term in enumerate((term_re, term_im, light * weight)):
                alone = pltpu.roll(jnp.where(lane // WIDTH == j, term, 0.0), shift, 1)
                for half, part in enumerate((jnp.where(lane >= column, alone, 0.0), jnp.where(lane < column, alone, 0.0))):
                    totals[field, pl.ds(2 * row + half, WIDTH, stride=2), :] += part
    for parity in range(2):
        for half in range(2):
            lanes = slice(half * HALF, (half + 1) * HALF)
            for field in range(3):
                out[parity, field, :, lanes] = totals[field, pl.ds(2 * parity + half, SIDE // 2, stride=4), :]
            for part in range(2):
                out[parity, 3 + part, :, lanes] = objects[pl.ds(4 * parity + 2 * part + half, SIDE // 2, stride=8), :]


def projection(templates):
    gram = lax.dot_general(
        templates, templates, (((1,), (1,)), ((), ())), precision=HIGHEST, preferred_element_type=jnp.float32
    )
    table = jnp.concatenate(
        [gram, jnp.zeros((EDGES, ENERGIES - EDGES), jnp.float32), templates], axis=1
    )
    which = lax.broadcasted_iota(jnp.int32, table.shape, 0)
    for k in range(EDGES):
        pivot = table[k : k + 1, :] / table[k : k + 1, k : k + 1]
        table = jnp.where(which == k, pivot, table - table[:, k : k + 1] * pivot)
    return table[:, ENERGIES:]


def exchange_kernel(
    fields,
    templates_ref,
    fitted,
    coefficients,
    partner,
    spectra,
    values,
    answer,
    landed,
    arrivals,
    sems,
):
    me, core = lax.axis_index("ea"), lax.axis_index("ta")
    barrier = pltpu.get_barrier_semaphore()

    def peer_of(step):
        return lax.rem(me + 1 + step, ENERGIES)

    def greet(step, carry):
        pl.semaphore_signal(barrier, inc=1, device_id={"ea": peer_of(step)}, device_id_type=MESH)
        return carry

    pl.semaphore_signal(barrier, inc=1, device_id={"ta": 1 - core}, device_id_type=MESH)
    lax.fori_loop(0, ENERGIES - 1, greet, 0)
    pl.semaphore_wait(barrier, ENERGIES)

    swap = pltpu.make_async_remote_copy(
        src_ref=fields.at[1 - core, pl.ds(0, 3)],
        dst_ref=partner,
        send_sem=sems.at[0],
        recv_sem=sems.at[1],
        device_id={"ta": 1 - core},
        device_id_type=MESH,
    )
    swap.start()
    swap.wait()
    scale = fields[core, 2] + partner[2] + REGULARIZER
    for part in range(2):
        own = fields[core, 3 + part]
        spectra[:, part * SIDE : (part + 1) * SIDE] = own - (fields[core, part] + partner[part]) / scale

    def send_all(source, target, first):
        def send(step, carry):
            peer = peer_of(step)
            pltpu.make_async_remote_copy(
                src_ref=source.at[pl.ds(peer, 1)],
                dst_ref=target.at[pl.ds(me, 1)],
                send_sem=sems.at[first],
                recv_sem=sems.at[first + 1],
                device_id={"ea": peer},
                device_id_type=MESH,
            ).start()
            return carry

        lax.fori_loop(0, ENERGIES - 1, send, 0)
        target[pl.ds(me, 1), :] = source[pl.ds(me, 1), :]

    def wait_all(first):
        pltpu.make_async_remote_copy(
            src_ref=arrivals,
            dst_ref=arrivals,
            send_sem=sems.at[first],
            recv_sem=sems.at[first + 1],
            device_id={"ea": peer_of(0)},
            device_id_type=MESH,
        ).wait()

    send_all(spectra, values, 2)
    templates = templates_ref[...]
    project = projection(templates)
    wait_all(2)
    coefs = jnp.dot(project, values[...], precision=HIGHEST, preferred_element_type=jnp.float32)
    for part in range(2):
        coefficients[part] = coefs[:, part * SIDE : (part + 1) * SIDE]
    answer[...] = lax.dot_general(
        templates, coefs, (((0,), (0,)), ((), ())), precision=HIGHEST, preferred_element_type=jnp.float32
    )
    send_all(answer, landed, 4)
    wait_all(4)
    for part in range(2):
        fitted[part] = landed[:, part * SIDE : (part + 1) * SIDE]


def local(
    sample_inphase,
    sample_quadrature,
    beam_inphase,
    beam_quadrature,
    recorded_diffraction,
    window_corners,
    filled_tallies,
    absorption_templates,
):
    vmem = pl.BlockSpec(memory_space=pltpu.VMEM)
    smem = pl.BlockSpec(memory_space=pltpu.SMEM)
    fields = pl.pallas_call(
        slots_kernel,
        out_shape=jax.ShapeDtypeStruct((2, 5, SIDE // 2, SIDE), jnp.float32),
        in_specs=[smem, smem] + [vmem] * 9,
        out_specs=vmem,
        scratch_shapes=[
            pltpu.VMEM((4 * SIDE, HALF), jnp.float32),
            pltpu.VMEM((3, 2 * SIDE, HALF), jnp.float32),
        ],
        compiler_params=pltpu.CompilerParams(vmem_limit_bytes=VMEM_BYTES),
    )(
        window_corners[0, 0],
        filled_tallies,
        sample_inphase,
        sample_quadrature,
        beam_inphase,
        beam_quadrature,
        recorded_diffraction,
        *[jnp.asarray(table) for table in dft_matrices()],
    )
    rows = pltpu.VMEM((ENERGIES, 2 * SIDE), jnp.float32)
    fitted, coefficients = pl.pallas_call(
        exchange_kernel,
        out_shape=(
            jax.ShapeDtypeStruct((2, ENERGIES, SIDE), jnp.float32),
            jax.ShapeDtypeStruct((2, EDGES, SIDE), jnp.float32),
        ),
        in_specs=[vmem] * 2,
        out_specs=(vmem, vmem),
        scratch_shapes=[
            pltpu.VMEM((3, SIDE // 2, SIDE), jnp.float32),
            rows,
            rows,
            rows,
            rows,
            pltpu.VMEM((ENERGIES - 1, 1, 2 * SIDE), jnp.float32),
            pltpu.SemaphoreType.DMA((6,)),
        ],
        compiler_params=pltpu.CompilerParams(
            collective_id=0, has_side_effects=True, vmem_limit_bytes=VMEM_BYTES
        ),
    )(fields, absorption_templates)
    return (fitted[:, None, :, None, :], coefficients)


def solution(mesh):
    in_specs = (
        P("ea", None, None),
        P("ea", None, None),
        P("ea", None, None, None),
        P("ea", None, None, None),
        P("ea", "ta", None, None, None),
        P("ea", "ta", None, None),
        P("ea", "ta"),
        P(),
    )
    out_specs = (P(None, "ea", None, "ta", None), P(None, None, ("ea", "ta")))
    return jax.shard_map(local, mesh=mesh, in_specs=in_specs, out_specs=out_specs, check_vma=False)
```

```python
import functools

import jax
import jax.numpy as jnp
import numpy as np
from jax import lax
from jax.experimental import pallas as pl
from jax.experimental.pallas import tpu as pltpu
from jax.sharding import PartitionSpec as P

MESH = pl.DeviceIdType.MESH
HIGHEST = lax.Precision.HIGHEST
FLOOR_POWER = 0.5
REGULARIZER = 1.0
ENERGIES = 128
EDGES = 16
SIDE = 256
HALF = 128
WIDTH = 32
MODES = 3
SLOTS = 16
PER_GROUP = 4
GROUPS = SLOTS // PER_GROUP
BAND = MODES * WIDTH
LANES = PER_GROUP * WIDTH
VMEM_BYTES = 48 * 1024 * 1024


def split_table(table):
    high = table.astype(jnp.bfloat16)
    low = (table - high.astype(np.float32)).astype(jnp.bfloat16)
    return np.stack([high, low])


def dft_matrices():
    index = np.arange(WIDTH)
    angles = 2.0 * np.pi / WIDTH * (index[:, None] * index[None, :] % WIDTH)
    re, im = np.cos(angles) / np.sqrt(WIDTH), -np.sin(angles) / np.sqrt(WIDTH)
    tables = []
    for sign in (1.0, -1.0):
        b_re, b_im = (np.kron(np.eye(PER_GROUP), part) for part in (re, sign * im))
        l_re, l_im = (np.kron(np.eye(MODES), part) for part in (re, sign * im))
        right = np.block([[b_re, b_im], [-b_im, b_re]]).astype(np.float32)
        left = np.block([[l_re, -l_im], [l_im, l_re]]).astype(np.float32)
        tables += [split_table(right), split_table(left)]
    return tables


def halves(value):
    high = value.astype(jnp.bfloat16)
    return high, (value - high.astype(jnp.float32)).astype(jnp.bfloat16)


def product(a, b):
    dot = functools.partial(jnp.dot, preferred_element_type=jnp.float32)
    return dot(a[0], b[0]) + (dot(a[0], b[1]) + dot(a[1], b[0]))


def slot_terms(corners, tally, objects, p_re, p_im, intensity, right_f, left_f, right_b, left_b):
    probe_re = [jnp.concatenate([p_re[0, m]] * PER_GROUP, axis=1) for m in range(MODES)]
    probe_im = [jnp.concatenate([p_im[0, m]] * PER_GROUP, axis=1) for m in range(MODES)]
    light = sum(a * a + b * b for a, b in zip(probe_re, probe_im))
    lane = lax.broadcasted_iota(jnp.int32, (WIDTH, LANES), 1)

    bands = []
    for g in range(GROUPS):
        patch = [jnp.zeros((WIDTH, LANES), jnp.float32)] * 2
        for j in range(PER_GROUP):
            s = g * PER_GROUP + j
            row, column = corners[0, s], corners[1, s]
            shift = lax.rem(WIDTH * j + SIDE - column, HALF)
            for part in range(2):
                left, right = (objects[pl.ds(4 * row + 2 * part + half, WIDTH, stride=4), :] for half in range(2))
                rolled = pltpu.roll(jnp.where(lane >= column, left, right), shift, 1)
                patch[part] = jnp.where(lane // WIDTH == j, rolled, patch[part])
        exits_re = [a * patch[0] - b * patch[1] for a, b in zip(probe_re, probe_im)]
        exits_im = [a * patch[1] + b * patch[0] for a, b in zip(probe_re, probe_im)]
        bands.append(
            jnp.concatenate(
                [jnp.concatenate(exits_re, axis=0), jnp.concatenate(exits_im, axis=0)], axis=1
            )
        )
    wide = product(halves(jnp.concatenate(bands, axis=0)), (right_f[0], right_f[1]))
    tall = jnp.concatenate(
        [
            jnp.concatenate([wide[g * BAND : (g + 1) * BAND, h * LANES : (h + 1) * LANES] for g in range(GROUPS)], axis=1)
            for h in range(2)
        ],
        axis=0,
    )
    far = product((left_f[0], left_f[1]), halves(tall))
    power = sum(
        far[k * WIDTH : (k + 1) * WIDTH] * far[k * WIDTH : (k + 1) * WIDTH] for k in range(2 * MODES)
    )
    measured = jnp.concatenate([intensity[0, 0, s] for s in range(SLOTS)], axis=1)
    used = lax.broadcasted_iota(jnp.int32, (WIDTH, GROUPS * LANES), 1) // WIDTH < tally
    factor = jnp.where(used, 1.0 - jnp.sqrt(measured) / jnp.sqrt(jnp.maximum(power, FLOOR_POWER)), 0.0)
    corrected = far * jnp.concatenate([factor] * (2 * MODES), axis=0)
    tall = product((left_b[0], left_b[1]), halves(corrected))
    wide = jnp.concatenate(
        [
            jnp.concatenate([tall[h * BAND : (h + 1) * BAND, g * LANES : (g + 1) * LANES] for h in range(2)], axis=1)
            for g in range(GROUPS)
        ],
        axis=0,
    )
    back = product(halves(wide), (right_b[0], right_b[1]))
    placed = []
    for g in range(GROUPS):
        term_re, term_im = jnp.zeros((2, WIDTH, LANES), jnp.float32)
        for m in range(MODES):
            rows = slice(g * BAND + m * WIDTH, g * BAND + (m + 1) * WIDTH)
            b_re, b_im = back[rows, :LANES], back[rows, LANES:]
            term_re += probe_re[m] * b_re + probe_im[m] * b_im
            term_im += probe_re[m] * b_im - probe_im[m] * b_re
        for j in range(PER_GROUP):
            s = g * PER_GROUP + j
            column = corners[1, s]
            shift = lax.rem(column + HALF - WIDTH * j, HALF)
            weight = jnp.where(s < tally, 1.0, 0.0)
            parts = []
            for term in (term_re, term_im, light * weight):
                alone = pltpu.roll(jnp.where(lane // WIDTH == j, term, 0.0), shift, 1)
                parts += [jnp.where(lane >= column, alone, 0.0), jnp.where(lane < column, alone, 0.0)]
            placed.append(jnp.concatenate(parts, axis=1))
    return jnp.concatenate(placed, axis=0)


def row_choice(corners, parity):
    lane = lax.broadcasted_iota(jnp.int32, (HALF, LANES), 1)
    row = 2 * lax.broadcasted_iota(jnp.int32, (HALF, LANES), 0) + parity
    choices = []
    for g in range(GROUPS):
        first = jnp.zeros((HALF, LANES), jnp.int32)
        for j in range(PER_GROUP):
            first = jnp.where(lane // WIDTH == j, corners[0, g * PER_GROUP + j] - WIDTH * j, first)
        choices.append(jnp.where(row == first + lane, 1.0, 0.0).astype(jnp.bfloat16))
    return jnp.concatenate(choices, axis=1)


def projection(templates):
    gram = lax.dot_general(
        templates, templates, (((1,), (1,)), ((), ())), precision=HIGHEST, preferred_element_type=jnp.float32
    )
    table = jnp.concatenate(
        [gram, jnp.zeros((EDGES, ENERGIES - EDGES), jnp.float32), templates], axis=1
    )
    which = lax.broadcasted_iota(jnp.int32, table.shape, 0)
    for k in range(EDGES):
        pivot = table[k : k + 1, :] / table[k : k + 1, k : k + 1]
        table = jnp.where(which == k, pivot, table - table[:, k : k + 1] * pivot)
    return table[:, ENERGIES:]


def step_kernel(
    corners,
    tallies,
    *refs,
):
    sources, (fitted, coefficients), (
        o_re,
        o_im,
        p_re,
        p_im,
        intensity,
        right_f,
        left_f,
        right_b,
        left_b,
        templates_ref,
        objects,
        away,
        partner,
        spectra,
        values,
        answer,
        arrivals,
        local_sems,
        sems,
    ) = refs[:SOURCES], refs[SOURCES : SOURCES + 2], refs[SOURCES + 2 :]
    me, core = lax.axis_index("ea"), lax.axis_index("ta")
    copies = [
        pltpu.make_async_copy(source, target, local_sems.at[k])
        for k, (source, target) in enumerate(
            zip(
                sources,
                (o_re, o_im, p_re, p_im, intensity, right_f, left_f, right_b, left_b, templates_ref),
            )
        )
    ]
    for copy in copies:
        copy.start()
    barrier = pltpu.get_barrier_semaphore()

    def peer_of(step):
        return lax.rem(me + 1 + step, ENERGIES)

    def greet(step, carry):
        pl.semaphore_signal(barrier, inc=1, device_id={"ea": peer_of(step)}, device_id_type=MESH)
        return carry

    pl.semaphore_signal(barrier, inc=1, device_id={"ta": 1 - core}, device_id_type=MESH)
    lax.fori_loop(0, ENERGIES - 1, greet, 0)
    for copy in copies:
        copy.wait()
    for part, source in enumerate((o_re, o_im)):
        for half in range(2):
            lanes = slice(half * HALF, (half + 1) * HALF)
            objects[pl.ds(2 * part + half, SIDE, stride=4), :] = source[0, :, lanes]
    placed = halves(
        slot_terms(corners, tallies[0, 0], objects, p_re, p_im, intensity, right_f, left_f, right_b, left_b)
    )

    def summed(parity):
        choice = row_choice(corners, parity)
        dot = functools.partial(jnp.dot, preferred_element_type=jnp.float32)
        return dot(choice, placed[0]) + dot(choice, placed[1])

    away[...] = summed(1 - core)
    pl.semaphore_wait(barrier, ENERGIES)
    swap = pltpu.make_async_remote_copy(
        src_ref=away,
        dst_ref=partner,
        send_sem=sems.at[0],
        recv_sem=sems.at[1],
        device_id={"ta": 1 - core},
        device_id_type=MESH,
    )
    swap.start()
    here = summed(core)
    swap.wait()
    scale = here[:, 2 * SIDE :] + partner[:, 2 * SIDE :] + REGULARIZER
    for part in range(2):
        lanes = slice(part * SIDE, (part + 1) * SIDE)
        own = jnp.concatenate(
            [objects[pl.ds(4 * core + 2 * part + half, HALF, stride=8), :] for half in range(2)], axis=1
        )
        spectra[part] = own - (here[:, lanes] + partner[:, lanes]) / scale

    def send_all(source, target, part, first):
        def send(step, carry):
            peer = peer_of(step)
            pltpu.make_async_remote_copy(
                src_ref=source.at[part, pl.ds(peer, 1)],
                dst_ref=target.at[part, pl.ds(me, 1)],
                send_sem=sems.at[first],
                recv_sem=sems.at[first + 1],
                device_id={"ea": peer},
                device_id_type=MESH,
            ).start()
            return carry

        lax.fori_loop(0, ENERGIES - 1, send, 0)
        target[part, pl.ds(me, 1), :] = source[part, pl.ds(me, 1), :]

    def wait_all(first):
        pltpu.make_async_remote_copy(
            src_ref=arrivals,
            dst_ref=arrivals,
            send_sem=sems.at[first],
            recv_sem=sems.at[first + 1],
            device_id={"ea": peer_of(0)},
            device_id_type=MESH,
        ).wait()

    for part in range(2):
        send_all(spectra, values, part, 2 + 2 * part)
    templates = templates_ref[...]
    project = projection(templates)
    for part in range(2):
        wait_all(2 + 2 * part)
        coefs = jnp.dot(project, values[part], precision=HIGHEST, preferred_element_type=jnp.float32)
        coefficients[part] = coefs
        answer[part] = lax.dot_general(
            templates, coefs, (((0,), (0,)), ((), ())), precision=HIGHEST, preferred_element_type=jnp.float32
        )
        send_all(answer, fitted, part, 6 + 2 * part)
    for part in range(2):
        wait_all(6 + 2 * part)


SOURCES = 10


def local(
    sample_inphase,
    sample_quadrature,
    beam_inphase,
    beam_quadrature,
    recorded_diffraction,
    window_corners,
    filled_tallies,
    absorption_templates,
):
    vmem = pl.BlockSpec(memory_space=pltpu.VMEM)
    smem = pl.BlockSpec(memory_space=pltpu.SMEM)
    sources = (
        sample_inphase,
        sample_quadrature,
        beam_inphase,
        beam_quadrature,
        recorded_diffraction,
        *[jnp.asarray(table) for table in dft_matrices()],
        absorption_templates,
    )
    rows = pltpu.VMEM((2, ENERGIES, SIDE), jnp.float32)
    fitted, coefficients = pl.pallas_call(
        step_kernel,
        out_shape=(
            jax.ShapeDtypeStruct((2, ENERGIES, SIDE), jnp.float32),
            jax.ShapeDtypeStruct((2, EDGES, SIDE), jnp.float32),
        ),
        in_specs=[smem, smem] + [pl.BlockSpec(memory_space=pl.ANY)] * SOURCES,
        out_specs=(vmem, vmem),
        scratch_shapes=[pltpu.VMEM(source.shape, source.dtype) for source in sources]
        + [
            pltpu.VMEM((4 * SIDE, HALF), jnp.float32),
            pltpu.VMEM((HALF, 3 * SIDE), jnp.float32),
            pltpu.VMEM((HALF, 3 * SIDE), jnp.float32),
            rows,
            rows,
            rows,
            pltpu.VMEM((ENERGIES - 1, 1, SIDE), jnp.float32),
            pltpu.SemaphoreType.DMA((SOURCES,)),
            pltpu.SemaphoreType.DMA((10,)),
        ],
        compiler_params=pltpu.CompilerParams(
            collective_id=0, has_side_effects=True, vmem_limit_bytes=VMEM_BYTES
        ),
    )(window_corners[0, 0].T, filled_tallies, *sources)
    return (fitted[:, None, :, None, :], coefficients)


def solution(mesh):
    in_specs = (
        P("ea", None, None),
        P("ea", None, None),
        P("ea", None, None, None),
        P("ea", None, None, None),
        P("ea", "ta", None, None, None),
        P("ea", "ta", None, None),
        P("ea", "ta"),
        P(),
    )
    out_specs = (P(None, "ea", None, "ta", None), P(None, None, ("ea", "ta")))
    return jax.shard_map(local, mesh=mesh, in_specs=in_specs, out_specs=out_specs, check_vma=False)
```

```python
import functools

import jax
import jax.numpy as jnp
import numpy as np
from jax import lax
from jax.experimental import pallas as pl
from jax.experimental.pallas import tpu as pltpu
from jax.sharding import PartitionSpec as P

MESH = pl.DeviceIdType.MESH
HIGHEST = lax.Precision.HIGHEST
FLOOR_POWER = 0.5
REGULARIZER = 1.0
ENERGIES = 128
EDGES = 16
SIDE = 256
HALF = 128
WIDTH = 32
MODES = 3
SLOTS = 16
PER_GROUP = 4
GROUPS = SLOTS // PER_GROUP
BAND = MODES * WIDTH
LANES = PER_GROUP * WIDTH
VMEM_BYTES = 54 * 1024 * 1024


def split_table(table):
    high = table.astype(jnp.bfloat16)
    low = (table - high.astype(np.float32)).astype(jnp.bfloat16)
    return np.stack([high, low])


def dft_matrices():
    index = np.arange(WIDTH)
    angles = 2.0 * np.pi / WIDTH * (index[:, None] * index[None, :] % WIDTH)
    re, im = np.cos(angles) / np.sqrt(WIDTH), -np.sin(angles) / np.sqrt(WIDTH)
    tables = []
    for sign in (1.0, -1.0):
        b_re, b_im = (np.kron(np.eye(PER_GROUP), part) for part in (re, sign * im))
        l_re, l_im = (np.kron(np.eye(MODES), part) for part in (re, sign * im))
        right = np.block([[b_re, b_im], [-b_im, b_re]]).astype(np.float32)
        left = np.block([[l_re, -l_im], [l_im, l_re]]).astype(np.float32)
        tables += [split_table(right), split_table(left)]
    return tables


def halves(value):
    high = value.astype(jnp.bfloat16)
    return high, (value - high.astype(jnp.float32)).astype(jnp.bfloat16)


def product(a, b):
    dot = functools.partial(jnp.dot, preferred_element_type=jnp.float32)
    return dot(a[0], b[0]) + (dot(a[0], b[1]) + dot(a[1], b[0]))


def slot_terms(corners, tally, objects, p_re, p_im, intensity, right_f, left_f, right_b, left_b):
    probe_re = [jnp.concatenate([p_re[0, m]] * PER_GROUP, axis=1) for m in range(MODES)]
    probe_im = [jnp.concatenate([p_im[0, m]] * PER_GROUP, axis=1) for m in range(MODES)]
    light = sum(a * a + b * b for a, b in zip(probe_re, probe_im))
    lane = lax.broadcasted_iota(jnp.int32, (WIDTH, LANES), 1)

    bands = []
    for g in range(GROUPS):
        patch = [jnp.zeros((WIDTH, LANES), jnp.float32)] * 2
        for j in range(PER_GROUP):
            s = g * PER_GROUP + j
            row, column = corners[0, s], corners[1, s]
            shift = lax.rem(WIDTH * j + SIDE - column, HALF)
            for part in range(2):
                left, right = (objects[pl.ds(4 * row + 2 * part + half, WIDTH, stride=4), :] for half in range(2))
                rolled = pltpu.roll(jnp.where(lane >= column, left, right), shift, 1)
                patch[part] = jnp.where(lane // WIDTH == j, rolled, patch[part])
        exits_re = [a * patch[0] - b * patch[1] for a, b in zip(probe_re, probe_im)]
        exits_im = [a * patch[1] + b * patch[0] for a, b in zip(probe_re, probe_im)]
        bands.append(
            jnp.concatenate(
                [jnp.concatenate(exits_re, axis=0), jnp.concatenate(exits_im, axis=0)], axis=1
            )
        )
    wide = product(halves(jnp.concatenate(bands, axis=0)), (right_f[0], right_f[1]))
    tall = jnp.concatenate(
        [
            jnp.concatenate([wide[g * BAND : (g + 1) * BAND, h * LANES : (h + 1) * LANES] for g in range(GROUPS)], axis=1)
            for h in range(2)
        ],
        axis=0,
    )
    far = product((left_f[0], left_f[1]), halves(tall))
    power = sum(
        far[k * WIDTH : (k + 1) * WIDTH] * far[k * WIDTH : (k + 1) * WIDTH] for k in range(2 * MODES)
    )
    measured = jnp.concatenate([intensity[0, 0, s] for s in range(SLOTS)], axis=1)
    used = lax.broadcasted_iota(jnp.int32, (WIDTH, GROUPS * LANES), 1) // WIDTH < tally
    factor = jnp.where(used, 1.0 - jnp.sqrt(measured) / jnp.sqrt(jnp.maximum(power, FLOOR_POWER)), 0.0)
    corrected = far * jnp.concatenate([factor] * (2 * MODES), axis=0)
    tall = product((left_b[0], left_b[1]), halves(corrected))
    wide = jnp.concatenate(
        [
            jnp.concatenate([tall[h * BAND : (h + 1) * BAND, g * LANES : (g + 1) * LANES] for h in range(2)], axis=1)
            for g in range(GROUPS)
        ],
        axis=0,
    )
    back = product(halves(wide), (right_b[0], right_b[1]))
    placed = []
    for g in range(GROUPS):
        term_re, term_im = jnp.zeros((2, WIDTH, LANES), jnp.float32)
        for m in range(MODES):
            rows = slice(g * BAND + m * WIDTH, g * BAND + (m + 1) * WIDTH)
            b_re, b_im = back[rows, :LANES], back[rows, LANES:]
            term_re += probe_re[m] * b_re + probe_im[m] * b_im
            term_im += probe_re[m] * b_im - probe_im[m] * b_re
        for j in range(PER_GROUP):
            s = g * PER_GROUP + j
            column = corners[1, s]
            shift = lax.rem(column + HALF - WIDTH * j, HALF)
            weight = jnp.where(s < tally, 1.0, 0.0)
            parts = []
            for term in (term_re, term_im, light * weight):
                alone = pltpu.roll(jnp.where(lane // WIDTH == j, term, 0.0), shift, 1)
                parts += [jnp.where(lane >= column, alone, 0.0), jnp.where(lane < column, alone, 0.0)]
            placed.append(jnp.concatenate(parts, axis=1))
    return jnp.concatenate(placed, axis=0)


def row_choice(corners, parity):
    lane = lax.broadcasted_iota(jnp.int32, (HALF, LANES), 1)
    row = 2 * lax.broadcasted_iota(jnp.int32, (HALF, LANES), 0) + parity
    choices = []
    for g in range(GROUPS):
        first = jnp.zeros((HALF, LANES), jnp.int32)
        for j in range(PER_GROUP):
            first = jnp.where(lane // WIDTH == j, corners[0, g * PER_GROUP + j] - WIDTH * j, first)
        choices.append(jnp.where(row == first + lane, 1.0, 0.0).astype(jnp.bfloat16))
    return jnp.concatenate(choices, axis=1)


def projection(templates):
    gram = lax.dot_general(
        templates, templates, (((1,), (1,)), ((), ())), precision=HIGHEST, preferred_element_type=jnp.float32
    )
    table = jnp.concatenate(
        [gram, jnp.zeros((EDGES, ENERGIES - EDGES), jnp.float32), templates], axis=1
    )
    which = lax.broadcasted_iota(jnp.int32, table.shape, 0)
    for k in range(EDGES):
        pivot = table[k : k + 1, :] / table[k : k + 1, k : k + 1]
        table = jnp.where(which == k, pivot, table - table[:, k : k + 1] * pivot)
    return table[:, ENERGIES:]


def step_kernel(
    corners,
    tallies,
    *refs,
):
    sources, (fitted, coefficients), (
        o_re,
        o_im,
        p_re,
        p_im,
        intensity,
        right_f,
        left_f,
        right_b,
        left_b,
        templates_ref,
        objects,
        away,
        partner,
        spectra,
        values,
        answer,
        arrivals,
        local_sems,
        sems,
    ) = refs[:SOURCES], refs[SOURCES : SOURCES + 2], refs[SOURCES + 2 :]
    me, core = lax.axis_index("ea"), lax.axis_index("ta")
    copies = [
        pltpu.make_async_copy(source, target, local_sems.at[k])
        for k, (source, target) in enumerate(
            zip(
                sources,
                (o_re, o_im, p_re, p_im, intensity, right_f, left_f, right_b, left_b, templates_ref),
            )
        )
    ]
    for copy in copies:
        copy.start()
    barrier = pltpu.get_barrier_semaphore()

    def peer_of(step):
        return lax.rem(me + 1 + step, ENERGIES)

    def greet(step, carry):
        pl.semaphore_signal(barrier, inc=1, device_id={"ea": peer_of(step)}, device_id_type=MESH)
        return carry

    pl.semaphore_signal(barrier, inc=1, device_id={"ta": 1 - core}, device_id_type=MESH)
    lax.fori_loop(0, ENERGIES - 1, greet, 0)
    for copy in copies:
        copy.wait()
    for part, source in enumerate((o_re, o_im)):
        for half in range(2):
            lanes = slice(half * HALF, (half + 1) * HALF)
            objects[pl.ds(2 * part + half, SIDE, stride=4), :] = source[0, :, lanes]
    placed = halves(
        slot_terms(corners, tallies[0, 0], objects, p_re, p_im, intensity, right_f, left_f, right_b, left_b)
    )

    def summed(parity):
        choice = row_choice(corners, parity)
        dot = functools.partial(jnp.dot, preferred_element_type=jnp.float32)
        return dot(choice, placed[0]) + dot(choice, placed[1])

    away[...] = summed(1 - core)
    pl.semaphore_wait(barrier, ENERGIES)
    swap = pltpu.make_async_remote_copy(
        src_ref=away,
        dst_ref=partner,
        send_sem=sems.at[0],
        recv_sem=sems.at[1],
        device_id={"ta": 1 - core},
        device_id_type=MESH,
    )
    swap.start()
    here = summed(core)
    swap.wait()
    scale = here[:, 2 * SIDE :] + partner[:, 2 * SIDE :] + REGULARIZER
    for part in range(2):
        lanes = slice(part * SIDE, (part + 1) * SIDE)
        own = jnp.concatenate(
            [objects[pl.ds(4 * core + 2 * part + half, HALF, stride=8), :] for half in range(2)], axis=1
        )
        spectra[part] = own - (here[:, lanes] + partner[:, lanes]) / scale

    x, y, depth = lax.rem(me, 4), me // 32, lax.rem(me // 4, 8)
    place = (y * 4 + lax.rem(depth, 4)) * 4 + x

    def send_one(source, target, part, first, peer):
        pltpu.make_async_remote_copy(
            src_ref=source.at[part, pl.ds(peer, 1)],
            dst_ref=target.at[part, pl.ds(me, 1)],
            send_sem=sems.at[first],
            recv_sem=sems.at[first + 1],
            device_id={"ea": peer},
            device_id_type=MESH,
        ).start()

    def send_all(source, target, part, first):
        def send(step, carry):
            send_one(source, target, part, first, peer_of(step))
            return carry

        lax.fori_loop(0, ENERGIES - 1, send, 0, unroll=8)
        target[part, pl.ds(me, 1), :] = source[part, pl.ds(me, 1), :]

    def send_side(source, target, part, first, side):
        def send(step, carry):
            spot = lax.rem(place + step, 64)
            peer = (spot // 16) * 32 + side * 16 + lax.rem(spot, 16)
            send_one(source, target, part, first, peer)
            return carry

        if side == 0:
            across = (y * 8 + lax.rem(depth + 4, 8)) * 4 + x
            send_one(source, target, part, first, across)
            target[part, pl.ds(me, 1), :] = source[part, pl.ds(me, 1), :]
        lax.fori_loop(1, 64, send, 0, unroll=9)

    def wait_all(first):
        pltpu.make_async_remote_copy(
            src_ref=arrivals,
            dst_ref=arrivals,
            send_sem=sems.at[first],
            recv_sem=sems.at[first + 1],
            device_id={"ea": peer_of(0)},
            device_id_type=MESH,
        ).wait()

    for part in range(2):
        send_all(spectra, values, part, 2 + 2 * part)
    templates = templates_ref[...]
    project = projection(templates)
    rebuild = lax.dot_general(
        templates, project, (((0,), (0,)), ((), ())), precision=HIGHEST, preferred_element_type=jnp.float32
    )
    solve = jnp.concatenate([rebuild, project], axis=0)
    for part in range(2):
        wait_all(2 + 2 * part)
        both = jnp.dot(solve, values[part], precision=HIGHEST, preferred_element_type=jnp.float32)
        answer[part] = both[:ENERGIES]
        coefficients[part] = both[ENERGIES:]
        for side in range(2):
            send_side(answer, fitted, part, 6 + 2 * part, side)
    for part in range(2):
        wait_all(6 + 2 * part)


SOURCES = 10


def local(
    sample_inphase,
    sample_quadrature,
    beam_inphase,
    beam_quadrature,
    recorded_diffraction,
    window_corners,
    filled_tallies,
    absorption_templates,
):
    vmem = pl.BlockSpec(memory_space=pltpu.VMEM)
    smem = pl.BlockSpec(memory_space=pltpu.SMEM)
    sources = (
        sample_inphase,
        sample_quadrature,
        beam_inphase,
        beam_quadrature,
        recorded_diffraction,
        *[jnp.asarray(table) for table in dft_matrices()],
        absorption_templates,
    )
    rows = pltpu.VMEM((2, ENERGIES, SIDE), jnp.float32)
    fitted, coefficients = pl.pallas_call(
        step_kernel,
        out_shape=(
            jax.ShapeDtypeStruct((2, ENERGIES, SIDE), jnp.float32),
            jax.ShapeDtypeStruct((2, EDGES, SIDE), jnp.float32),
        ),
        in_specs=[smem, smem] + [pl.BlockSpec(memory_space=pl.ANY)] * SOURCES,
        out_specs=(vmem, vmem),
        scratch_shapes=[pltpu.VMEM(source.shape, source.dtype) for source in sources]
        + [
            pltpu.VMEM((4 * SIDE, HALF), jnp.float32),
            pltpu.VMEM((HALF, 3 * SIDE), jnp.float32),
            pltpu.VMEM((HALF, 3 * SIDE), jnp.float32),
            rows,
            rows,
            rows,
            pltpu.VMEM((ENERGIES - 1, 1, SIDE), jnp.float32),
            pltpu.SemaphoreType.DMA((SOURCES,)),
            pltpu.SemaphoreType.DMA((10,)),
        ],
        compiler_params=pltpu.CompilerParams(
            collective_id=0, has_side_effects=True, vmem_limit_bytes=VMEM_BYTES
        ),
    )(window_corners[0, 0].T, filled_tallies, *sources)
    return (fitted[:, None, :, None, :], coefficients)


def solution(mesh):
    in_specs = (
        P("ea", None, None),
        P("ea", None, None),
        P("ea", None, None, None),
        P("ea", None, None, None),
        P("ea", "ta", None, None, None),
        P("ea", "ta", None, None),
        P("ea", "ta"),
        P(),
    )
    out_specs = (P(None, "ea", None, "ta", None), P(None, None, ("ea", "ta")))
    return jax.shard_map(local, mesh=mesh, in_specs=in_specs, out_specs=out_specs, check_vma=False)
```

```python
import functools

import jax
import jax.numpy as jnp
import numpy as np
from jax import lax
from jax.experimental import pallas as pl
from jax.experimental.pallas import tpu as pltpu
from jax.sharding import PartitionSpec as P

MESH = pl.DeviceIdType.MESH
HIGHEST = lax.Precision.HIGHEST
FLOOR_POWER = 0.5
REGULARIZER = 1.0
ENERGIES = 128
EDGES = 16
SIDE = 256
HALF = 128
WIDTH = 32
MODES = 3
SLOTS = 16
PER_GROUP = 4
GROUPS = SLOTS // PER_GROUP
BAND = MODES * WIDTH
LANES = PER_GROUP * WIDTH
VMEM_BYTES = 54 * 1024 * 1024


def split_table(table):
    high = table.astype(jnp.bfloat16)
    low = (table - high.astype(np.float32)).astype(jnp.bfloat16)
    return np.stack([high, low])


def dft_matrices():
    index = np.arange(WIDTH)
    angles = 2.0 * np.pi / WIDTH * (index[:, None] * index[None, :] % WIDTH)
    re, im = np.cos(angles) / np.sqrt(WIDTH), -np.sin(angles) / np.sqrt(WIDTH)
    tables = []
    for sign in (1.0, -1.0):
        b_re, b_im = (np.kron(np.eye(PER_GROUP), part) for part in (re, sign * im))
        l_re, l_im = (np.kron(np.eye(MODES), part) for part in (re, sign * im))
        right = np.block([[b_re, b_im], [-b_im, b_re]]).astype(np.float32)
        left = np.block([[l_re, -l_im], [l_im, l_re]]).astype(np.float32)
        tables += [split_table(right), split_table(left)]
    return tables


def halves(value):
    high = value.astype(jnp.bfloat16)
    return high, (value - high.astype(jnp.float32)).astype(jnp.bfloat16)


def product(a, b):
    dot = functools.partial(jnp.dot, preferred_element_type=jnp.float32)
    return dot(a[0], b[0]) + (dot(a[0], b[1]) + dot(a[1], b[0]))


def slot_terms(corners, tally, objects, p_re, p_im, intensity, right_f, left_f, right_b, left_b):
    probe_re = [jnp.concatenate([p_re[0, m]] * PER_GROUP, axis=1) for m in range(MODES)]
    probe_im = [jnp.concatenate([p_im[0, m]] * PER_GROUP, axis=1) for m in range(MODES)]
    light = sum(a * a + b * b for a, b in zip(probe_re, probe_im))
    lane = lax.broadcasted_iota(jnp.int32, (WIDTH, LANES), 1)

    bands = []
    for g in range(GROUPS):
        patch = [jnp.zeros((WIDTH, LANES), jnp.float32)] * 2
        for j in range(PER_GROUP):
            s = g * PER_GROUP + j
            row, column = corners[0, s], corners[1, s]
            shift = lax.rem(WIDTH * j + SIDE - column, HALF)
            for part in range(2):
                left, right = (objects[pl.ds(4 * row + 2 * part + half, WIDTH, stride=4), :] for half in range(2))
                rolled = pltpu.roll(jnp.where(lane >= column, left, right), shift, 1)
                patch[part] = jnp.where(lane // WIDTH == j, rolled, patch[part])
        exits_re = [a * patch[0] - b * patch[1] for a, b in zip(probe_re, probe_im)]
        exits_im = [a * patch[1] + b * patch[0] for a, b in zip(probe_re, probe_im)]
        bands.append(
            jnp.concatenate(
                [jnp.concatenate(exits_re, axis=0), jnp.concatenate(exits_im, axis=0)], axis=1
            )
        )
    wide = product(halves(jnp.concatenate(bands, axis=0)), (right_f[0], right_f[1]))
    tall = jnp.concatenate(
        [
            jnp.concatenate([wide[g * BAND : (g + 1) * BAND, h * LANES : (h + 1) * LANES] for g in range(GROUPS)], axis=1)
            for h in range(2)
        ],
        axis=0,
    )
    far = product((left_f[0], left_f[1]), halves(tall))
    power = sum(
        far[k * WIDTH : (k + 1) * WIDTH] * far[k * WIDTH : (k + 1) * WIDTH] for k in range(2 * MODES)
    )
    measured = jnp.concatenate([intensity[0, 0, s] for s in range(SLOTS)], axis=1)
    used = lax.broadcasted_iota(jnp.int32, (WIDTH, GROUPS * LANES), 1) // WIDTH < tally
    factor = jnp.where(used, 1.0 - jnp.sqrt(measured) / jnp.sqrt(jnp.maximum(power, FLOOR_POWER)), 0.0)
    corrected = far * jnp.concatenate([factor] * (2 * MODES), axis=0)
    tall = product((left_b[0], left_b[1]), halves(corrected))
    wide = jnp.concatenate(
        [
            jnp.concatenate([tall[h * BAND : (h + 1) * BAND, g * LANES : (g + 1) * LANES] for h in range(2)], axis=1)
            for g in range(GROUPS)
        ],
        axis=0,
    )
    back = product(halves(wide), (right_b[0], right_b[1]))
    placed = []
    for g in range(GROUPS):
        term_re, term_im = jnp.zeros((2, WIDTH, LANES), jnp.float32)
        for m in range(MODES):
            rows = slice(g * BAND + m * WIDTH, g * BAND + (m + 1) * WIDTH)
            b_re, b_im = back[rows, :LANES], back[rows, LANES:]
            term_re += probe_re[m] * b_re + probe_im[m] * b_im
            term_im += probe_re[m] * b_im - probe_im[m] * b_re
        for j in range(PER_GROUP):
            s = g * PER_GROUP + j
            column = corners[1, s]
            shift = lax.rem(column + HALF - WIDTH * j, HALF)
            weight = jnp.where(s < tally, 1.0, 0.0)
            parts = []
            for term in (term_re, light * weight, term_im):
                alone = pltpu.roll(jnp.where(lane // WIDTH == j, term, 0.0), shift, 1)
                parts += [jnp.where(lane >= column, alone, 0.0), jnp.where(lane < column, alone, 0.0)]
            placed.append(jnp.concatenate(parts, axis=1))
    return jnp.concatenate(placed, axis=0)


def row_choice(corners, parity):
    lane = lax.broadcasted_iota(jnp.int32, (HALF, LANES), 1)
    row = 2 * lax.broadcasted_iota(jnp.int32, (HALF, LANES), 0) + parity
    choices = []
    for g in range(GROUPS):
        first = jnp.zeros((HALF, LANES), jnp.int32)
        for j in range(PER_GROUP):
            first = jnp.where(lane // WIDTH == j, corners[0, g * PER_GROUP + j] - WIDTH * j, first)
        choices.append(jnp.where(row == first + lane, 1.0, 0.0).astype(jnp.bfloat16))
    return jnp.concatenate(choices, axis=1)


def projection(templates):
    gram = lax.dot_general(
        templates, templates, (((1,), (1,)), ((), ())), precision=HIGHEST, preferred_element_type=jnp.float32
    )
    table = jnp.concatenate(
        [gram, jnp.zeros((EDGES, ENERGIES - EDGES), jnp.float32), templates], axis=1
    )
    which = lax.broadcasted_iota(jnp.int32, table.shape, 0)
    for k in range(EDGES):
        pivot = table[k : k + 1, :] / table[k : k + 1, k : k + 1]
        table = jnp.where(which == k, pivot, table - table[:, k : k + 1] * pivot)
    return table[:, ENERGIES:]


def step_kernel(
    corners,
    tallies,
    *refs,
):
    sources, (fitted, coefficients), (
        o_re,
        o_im,
        p_re,
        p_im,
        intensity,
        right_f,
        left_f,
        right_b,
        left_b,
        templates_ref,
        objects,
        away,
        partner,
        spectra,
        values,
        answer,
        arrivals,
        local_sems,
        sems,
    ) = refs[:SOURCES], refs[SOURCES : SOURCES + 2], refs[SOURCES + 2 :]
    me, core = lax.axis_index("ea"), lax.axis_index("ta")
    copies = [
        pltpu.make_async_copy(source, target, local_sems.at[k])
        for k, (source, target) in enumerate(
            zip(
                sources,
                (o_re, o_im, p_re, p_im, intensity, right_f, left_f, right_b, left_b, templates_ref),
            )
        )
    ]
    for copy in copies:
        copy.start()
    barrier = pltpu.get_barrier_semaphore()

    def peer_of(step):
        return lax.rem(me + 1 + step, ENERGIES)

    def greet(step, carry):
        pl.semaphore_signal(barrier, inc=1, device_id={"ea": peer_of(step)}, device_id_type=MESH)
        return carry

    pl.semaphore_signal(barrier, inc=1, device_id={"ta": 1 - core}, device_id_type=MESH)
    lax.fori_loop(0, ENERGIES - 1, greet, 0, unroll=8)
    for copy in copies:
        copy.wait()
    for part, source in enumerate((o_re, o_im)):
        for half in range(2):
            lanes = slice(half * HALF, (half + 1) * HALF)
            objects[pl.ds(2 * part + half, SIDE, stride=4), :] = source[0, :, lanes]
    placed = halves(
        slot_terms(corners, tallies[0, 0], objects, p_re, p_im, intensity, right_f, left_f, right_b, left_b)
    )

    def summed(choice, columns):
        dot = functools.partial(jnp.dot, preferred_element_type=jnp.float32)
        return dot(choice, placed[0][:, columns]) + dot(choice, placed[1][:, columns])

    def swap(lanes, first):
        return pltpu.make_async_remote_copy(
            src_ref=away.at[:, lanes],
            dst_ref=partner.at[:, lanes],
            send_sem=sems.at[first],
            recv_sem=sems.at[first + 1],
            device_id={"ta": 1 - core},
            device_id_type=MESH,
        )

    choice = row_choice(corners, 1 - core)
    firsts, seconds = slice(0, 2 * SIDE), slice(2 * SIDE, 3 * SIDE)
    swaps = [swap(pl.ds(0, 2 * SIDE), 0), swap(pl.ds(2 * SIDE, SIDE), 12)]
    away[:, firsts] = summed(choice, firsts)
    pl.semaphore_wait(barrier, ENERGIES)
    swaps[0].start()
    away[:, seconds] = summed(choice, seconds)
    swaps[1].start()
    choice = row_choice(corners, core)
    here = [summed(choice, firsts), summed(choice, seconds)]

    def update(part, total, scale):
        own = jnp.concatenate(
            [objects[pl.ds(4 * core + 2 * part + half, HALF, stride=8), :] for half in range(2)], axis=1
        )
        spectra[part] = own - total / scale

    x, y, depth = lax.rem(me, 4), me // 32, lax.rem(me // 4, 8)
    place = (y * 4 + lax.rem(depth, 4)) * 4 + x

    def landing(target, part):
        return target.at[part, pl.ds(me, 1)] if target is values else target.at[part, 0, me]

    def send_one(source, target, part, first, peer):
        pltpu.make_async_remote_copy(
            src_ref=source.at[part, pl.ds(peer, 1)],
            dst_ref=landing(target, part),
            send_sem=sems.at[first],
            recv_sem=sems.at[first + 1],
            device_id={"ea": peer},
            device_id_type=MESH,
        ).start()

    def send_all(source, target, part, first):
        def send(step, carry):
            send_one(source, target, part, first, peer_of(step))
            return carry

        lax.fori_loop(0, ENERGIES - 1, send, 0, unroll=8)
        target[part, pl.ds(me, 1), :] = source[part, pl.ds(me, 1), :]

    def keep(part):
        return pltpu.make_async_copy(answer.at[part, pl.ds(me, 1)], fitted.at[part, 0, me], sems.at[10 + part])

    def send_side(source, target, part, first, side):
        def send(step, carry):
            spot = lax.rem(place + step, 64)
            peer = (spot // 16) * 32 + side * 16 + lax.rem(spot, 16)
            send_one(source, target, part, first, peer)
            return carry

        if side == 0:
            across = (y * 8 + lax.rem(depth + 4, 8)) * 4 + x
            send_one(source, target, part, first, across)
            keep(part).start()
        lax.fori_loop(1, 64, send, 0, unroll=9)

    def wait_all(first):
        pltpu.make_async_remote_copy(
            src_ref=arrivals,
            dst_ref=arrivals,
            send_sem=sems.at[first],
            recv_sem=sems.at[first + 1],
            device_id={"ea": peer_of(0)},
            device_id_type=MESH,
        ).wait()

    swaps[0].wait()
    scale = here[0][:, SIDE:] + partner[:, SIDE : 2 * SIDE] + REGULARIZER
    update(0, here[0][:, :SIDE] + partner[:, :SIDE], scale)
    send_all(spectra, values, 0, 2)
    swaps[1].wait()
    update(1, here[1] + partner[:, seconds], scale)
    send_all(spectra, values, 1, 4)
    templates = templates_ref[...]
    project = projection(templates)
    rebuild = lax.dot_general(
        templates, project, (((0,), (0,)), ((), ())), precision=HIGHEST, preferred_element_type=jnp.float32
    )
    solve = jnp.concatenate([rebuild, project], axis=0)
    for part in range(2):
        wait_all(2 + 2 * part)
        both = jnp.dot(solve, values[part], precision=HIGHEST, preferred_element_type=jnp.float32)
        answer[part] = both[:ENERGIES]
        coefficients[part] = both[ENERGIES:]
        for side in range(2):
            send_side(answer, fitted, part, 6 + 2 * part, side)
    for part in range(2):
        wait_all(6 + 2 * part)
        keep(part).wait()


SOURCES = 10


def hand_on(fitted, coefficients, fitted_out, coefficients_out, fitted_held, coefficients_held, sems):
    stages = [
        (fitted.at[part], fitted_held.at[part], fitted_out.at[part]) for part in range(2)
    ] + [(coefficients, coefficients_held, coefficients_out)]
    into = [pltpu.make_async_copy(a, b, sems.at[0, k]) for k, (a, b, c) in enumerate(stages)]
    onward = [pltpu.make_async_copy(b, c, sems.at[1, k]) for k, (a, b, c) in enumerate(stages)]
    for copy in into:
        copy.start()
    for first, second in zip(into, onward):
        first.wait()
        second.start()
    for copy in onward:
        copy.wait()


def local(
    sample_inphase,
    sample_quadrature,
    beam_inphase,
    beam_quadrature,
    recorded_diffraction,
    window_corners,
    filled_tallies,
    absorption_templates,
):
    vmem = pl.BlockSpec(memory_space=pltpu.VMEM)
    smem = pl.BlockSpec(memory_space=pltpu.SMEM)
    sources = (
        sample_inphase,
        sample_quadrature,
        beam_inphase,
        beam_quadrature,
        recorded_diffraction,
        *[jnp.asarray(table) for table in dft_matrices()],
        absorption_templates,
    )
    rows = pltpu.VMEM((2, ENERGIES, SIDE), jnp.float32)
    fitted, coefficients = pl.pallas_call(
        step_kernel,
        out_shape=(
            jax.ShapeDtypeStruct((2, 1, ENERGIES, 1, SIDE), jnp.float32),
            jax.ShapeDtypeStruct((2, EDGES, SIDE), jnp.float32),
        ),
        in_specs=[smem, smem] + [pl.BlockSpec(memory_space=pl.ANY)] * SOURCES,
        out_specs=(pl.BlockSpec(memory_space=pl.ANY), vmem),
        scratch_shapes=[pltpu.VMEM(source.shape, source.dtype) for source in sources]
        + [
            pltpu.VMEM((4 * SIDE, HALF), jnp.float32),
            pltpu.VMEM((HALF, 3 * SIDE), jnp.float32),
            pltpu.VMEM((HALF, 3 * SIDE), jnp.float32),
            rows,
            rows,
            rows,
            pltpu.VMEM((ENERGIES - 1, 1, SIDE), jnp.float32),
            pltpu.SemaphoreType.DMA((SOURCES,)),
            pltpu.SemaphoreType.DMA((14,)),
        ],
        compiler_params=pltpu.CompilerParams(
            collective_id=0, has_side_effects=True, vmem_limit_bytes=VMEM_BYTES
        ),
    )(window_corners[0, 0].T, filled_tallies, *sources)
    whole = pl.BlockSpec(memory_space=pl.ANY)
    return pl.pallas_call(
        hand_on,
        out_shape=(
            jax.ShapeDtypeStruct(fitted.shape, jnp.float32),
            jax.ShapeDtypeStruct(coefficients.shape, jnp.float32),
        ),
        in_specs=[whole, whole],
        out_specs=(whole, whole),
        scratch_shapes=[
            pltpu.VMEM(fitted.shape, jnp.float32),
            pltpu.VMEM(coefficients.shape, jnp.float32),
            pltpu.SemaphoreType.DMA((2, 3)),
        ],
        compiler_params=pltpu.CompilerParams(vmem_limit_bytes=VMEM_BYTES),
    )(fitted, coefficients)


def solution(mesh):
    in_specs = (
        P("ea", None, None),
        P("ea", None, None),
        P("ea", None, None, None),
        P("ea", None, None, None),
        P("ea", "ta", None, None, None),
        P("ea", "ta", None, None),
        P("ea", "ta"),
        P(),
    )
    out_specs = (P(None, "ea", None, "ta", None), P(None, None, ("ea", "ta")))
    return jax.shard_map(local, mesh=mesh, in_specs=in_specs, out_specs=out_specs, check_vma=False)
```

```python
import functools

import jax
import jax.numpy as jnp
import numpy as np
from jax import lax
from jax.experimental import pallas as pl
from jax.experimental.pallas import tpu as pltpu
from jax.sharding import PartitionSpec as P

MESH = pl.DeviceIdType.MESH
HIGHEST = lax.Precision.HIGHEST
FLOOR_POWER = 0.5
REGULARIZER = 1.0
ENERGIES = 128
EDGES = 16
SIDE = 256
HALF = 128
WIDTH = 32
MODES = 3
SLOTS = 16
PER_GROUP = 4
GROUPS = SLOTS // PER_GROUP
BAND = MODES * WIDTH
LANES = PER_GROUP * WIDTH
VMEM_BYTES = 54 * 1024 * 1024


def split_table(table):
    high = table.astype(jnp.bfloat16)
    low = (table - high.astype(np.float32)).astype(jnp.bfloat16)
    return np.stack([high, low])


def dft_matrices():
    index = np.arange(WIDTH)
    angles = 2.0 * np.pi / WIDTH * (index[:, None] * index[None, :] % WIDTH)
    re, im = np.cos(angles) / np.sqrt(WIDTH), -np.sin(angles) / np.sqrt(WIDTH)
    tables = []
    for sign in (1.0, -1.0):
        b_re, b_im = (np.kron(np.eye(PER_GROUP), part) for part in (re, sign * im))
        l_re, l_im = (np.kron(np.eye(MODES), part) for part in (re, sign * im))
        right = np.block([[b_re, b_im], [-b_im, b_re]]).astype(np.float32)
        left = np.block([[l_re, -l_im], [l_im, l_re]]).astype(np.float32)
        tables += [split_table(right), split_table(left)]
    return tables


def halves(value):
    high = value.astype(jnp.bfloat16)
    return high, (value - high.astype(jnp.float32)).astype(jnp.bfloat16)


def product(a, b):
    dot = functools.partial(jnp.dot, preferred_element_type=jnp.float32)
    return dot(a[0], b[0]) + (dot(a[0], b[1]) + dot(a[1], b[0]))


def slot_terms(corners, tally, objects, p_re, p_im, intensity, right_f, left_f, right_b, left_b):
    probe_re = [jnp.concatenate([p_re[0, m]] * PER_GROUP, axis=1) for m in range(MODES)]
    probe_im = [jnp.concatenate([p_im[0, m]] * PER_GROUP, axis=1) for m in range(MODES)]
    light = sum(a * a + b * b for a, b in zip(probe_re, probe_im))
    lane = lax.broadcasted_iota(jnp.int32, (WIDTH, LANES), 1)

    bands = []
    for g in range(GROUPS):
        patch = [jnp.zeros((WIDTH, LANES), jnp.float32)] * 2
        for j in range(PER_GROUP):
            s = g * PER_GROUP + j
            row, column = corners[0, s], corners[1, s]
            shift = lax.rem(WIDTH * j + SIDE - column, HALF)
            for part in range(2):
                left, right = (objects[pl.ds(4 * row + 2 * part + half, WIDTH, stride=4), :] for half in range(2))
                rolled = pltpu.roll(jnp.where(lane >= column, left, right), shift, 1)
                patch[part] = jnp.where(lane // WIDTH == j, rolled, patch[part])
        exits_re = [a * patch[0] - b * patch[1] for a, b in zip(probe_re, probe_im)]
        exits_im = [a * patch[1] + b * patch[0] for a, b in zip(probe_re, probe_im)]
        bands.append(
            jnp.concatenate(
                [jnp.concatenate(exits_re, axis=0), jnp.concatenate(exits_im, axis=0)], axis=1
            )
        )
    wide = product(halves(jnp.concatenate(bands, axis=0)), (right_f[0], right_f[1]))
    tall = jnp.concatenate(
        [
            jnp.concatenate([wide[g * BAND : (g + 1) * BAND, h * LANES : (h + 1) * LANES] for g in range(GROUPS)], axis=1)
            for h in range(2)
        ],
        axis=0,
    )
    far = product((left_f[0], left_f[1]), halves(tall))
    power = sum(
        far[k * WIDTH : (k + 1) * WIDTH] * far[k * WIDTH : (k + 1) * WIDTH] for k in range(2 * MODES)
    )
    measured = jnp.concatenate([intensity[0, 0, s] for s in range(SLOTS)], axis=1)
    used = lax.broadcasted_iota(jnp.int32, (WIDTH, GROUPS * LANES), 1) // WIDTH < tally
    factor = jnp.where(used, 1.0 - jnp.sqrt(measured) / jnp.sqrt(jnp.maximum(power, FLOOR_POWER)), 0.0)
    corrected = far * jnp.concatenate([factor] * (2 * MODES), axis=0)
    tall = product((left_b[0], left_b[1]), halves(corrected))
    wide = jnp.concatenate(
        [
            jnp.concatenate([tall[h * BAND : (h + 1) * BAND, g * LANES : (g + 1) * LANES] for h in range(2)], axis=1)
            for g in range(GROUPS)
        ],
        axis=0,
    )
    back = product(halves(wide), (right_b[0], right_b[1]))
    placed = []
    for g in range(GROUPS):
        term_re, term_im = jnp.zeros((2, WIDTH, LANES), jnp.float32)
        for m in range(MODES):
            rows = slice(g * BAND + m * WIDTH, g * BAND + (m + 1) * WIDTH)
            b_re, b_im = back[rows, :LANES], back[rows, LANES:]
            term_re += probe_re[m] * b_re + probe_im[m] * b_im
            term_im += probe_re[m] * b_im - probe_im[m] * b_re
        for j in range(PER_GROUP):
            s = g * PER_GROUP + j
            column = corners[1, s]
            shift = lax.rem(column + HALF - WIDTH * j, HALF)
            weight = jnp.where(s < tally, 1.0, 0.0)
            parts = []
            for term in (term_re, light * weight, term_im):
                alone = pltpu.roll(jnp.where(lane // WIDTH == j, term, 0.0), shift, 1)
                parts += [jnp.where(lane >= column, alone, 0.0), jnp.where(lane < column, alone, 0.0)]
            placed.append(jnp.concatenate(parts, axis=1))
    return jnp.concatenate(placed, axis=0)


def row_choice(corners, parity):
    lane = lax.broadcasted_iota(jnp.int32, (HALF, LANES), 1)
    row = 2 * lax.broadcasted_iota(jnp.int32, (HALF, LANES), 0) + parity
    choices = []
    for g in range(GROUPS):
        first = jnp.zeros((HALF, LANES), jnp.int32)
        for j in range(PER_GROUP):
            first = jnp.where(lane // WIDTH == j, corners[0, g * PER_GROUP + j] - WIDTH * j, first)
        choices.append(jnp.where(row == first + lane, 1.0, 0.0).astype(jnp.bfloat16))
    return jnp.concatenate(choices, axis=1)


def projection(templates):
    gram = lax.dot_general(
        templates, templates, (((1,), (1,)), ((), ())), precision=HIGHEST, preferred_element_type=jnp.float32
    )
    table = jnp.concatenate(
        [gram, jnp.zeros((EDGES, ENERGIES - EDGES), jnp.float32), templates], axis=1
    )
    which = lax.broadcasted_iota(jnp.int32, table.shape, 0)
    for k in range(EDGES):
        pivot = table[k : k + 1, :] / table[k : k + 1, k : k + 1]
        table = jnp.where(which == k, pivot, table - table[:, k : k + 1] * pivot)
    return table[:, ENERGIES:]


def step_kernel(*refs):
    sources, (fitted, coefficients), (
        corners,
        tallies,
        o_re,
        o_im,
        p_re,
        p_im,
        intensity,
        right_f,
        left_f,
        right_b,
        left_b,
        templates_ref,
        objects,
        away,
        partner,
        spectra,
        values,
        answer,
        arrivals,
        local_sems,
        sems,
    ) = refs[:SOURCES], refs[SOURCES : SOURCES + 2], refs[SOURCES + 2 :]
    me, core = lax.axis_index("ea"), lax.axis_index("ta")
    copies = [
        pltpu.make_async_copy(source, target, local_sems.at[k])
        for k, (source, target) in enumerate(
            zip(
                sources,
                (corners, tallies, o_re, o_im, p_re, p_im, intensity, right_f, left_f, right_b, left_b, templates_ref),
            )
        )
    ]
    for copy in copies:
        copy.start()
    barrier = pltpu.get_barrier_semaphore()

    def peer_of(step):
        return lax.rem(me + 1 + step, ENERGIES)

    def greet(step, carry):
        pl.semaphore_signal(barrier, inc=1, device_id={"ea": peer_of(step)}, device_id_type=MESH)
        return carry

    pl.semaphore_signal(barrier, inc=1, device_id={"ta": 1 - core}, device_id_type=MESH)
    lax.fori_loop(0, ENERGIES - 1, greet, 0, unroll=8)
    for copy in copies:
        copy.wait()
    for part, source in enumerate((o_re, o_im)):
        for half in range(2):
            lanes = slice(half * HALF, (half + 1) * HALF)
            objects[pl.ds(2 * part + half, SIDE, stride=4), :] = source[0, :, lanes]
    placed = halves(
        slot_terms(corners, tallies[0, 0], objects, p_re, p_im, intensity, right_f, left_f, right_b, left_b)
    )

    def summed(choice, columns):
        dot = functools.partial(jnp.dot, preferred_element_type=jnp.float32)
        return dot(choice, placed[0][:, columns]) + dot(choice, placed[1][:, columns])

    def swap(lanes, first):
        return pltpu.make_async_remote_copy(
            src_ref=away.at[:, lanes],
            dst_ref=partner.at[:, lanes],
            send_sem=sems.at[first],
            recv_sem=sems.at[first + 1],
            device_id={"ta": 1 - core},
            device_id_type=MESH,
        )

    choice = row_choice(corners, 1 - core)
    firsts, seconds = slice(0, 2 * SIDE), slice(2 * SIDE, 3 * SIDE)
    swaps = [swap(pl.ds(0, 2 * SIDE), 0), swap(pl.ds(2 * SIDE, SIDE), 12)]
    away[:, firsts] = summed(choice, firsts)
    pl.semaphore_wait(barrier, ENERGIES)
    swaps[0].start()
    away[:, seconds] = summed(choice, seconds)
    swaps[1].start()
    choice = row_choice(corners, core)
    here = [summed(choice, firsts), summed(choice, seconds)]

    def update(part, total, scale):
        own = jnp.concatenate(
            [objects[pl.ds(4 * core + 2 * part + half, HALF, stride=8), :] for half in range(2)], axis=1
        )
        spectra[part] = own - total / scale

    x, y, depth = lax.rem(me, 4), me // 32, lax.rem(me // 4, 8)
    place = (y * 4 + lax.rem(depth, 4)) * 4 + x

    def landing(target, part):
        return target.at[part, pl.ds(me, 1)] if target is values else target.at[part, 0, me]

    def send_one(source, target, part, first, peer):
        pltpu.make_async_remote_copy(
            src_ref=source.at[part, pl.ds(peer, 1)],
            dst_ref=landing(target, part),
            send_sem=sems.at[first],
            recv_sem=sems.at[first + 1],
            device_id={"ea": peer},
            device_id_type=MESH,
        ).start()

    def send_all(source, target, part, first):
        def send(step, carry):
            send_one(source, target, part, first, peer_of(step))
            return carry

        lax.fori_loop(0, ENERGIES - 1, send, 0, unroll=8)
        target[part, pl.ds(me, 1), :] = source[part, pl.ds(me, 1), :]

    def keep(part):
        return pltpu.make_async_copy(answer.at[part, pl.ds(me, 1)], fitted.at[part, 0, me], sems.at[10 + part])

    def send_side(source, target, part, first, side):
        def send(step, carry):
            spot = lax.rem(place + step, 64)
            peer = (spot // 16) * 32 + side * 16 + lax.rem(spot, 16)
            send_one(source, target, part, first, peer)
            return carry

        if side == 0:
            across = (y * 8 + lax.rem(depth + 4, 8)) * 4 + x
            send_one(source, target, part, first, across)
            keep(part).start()
        lax.fori_loop(1, 64, send, 0, unroll=9)

    def wait_all(first):
        pltpu.make_async_remote_copy(
            src_ref=arrivals,
            dst_ref=arrivals,
            send_sem=sems.at[first],
            recv_sem=sems.at[first + 1],
            device_id={"ea": peer_of(0)},
            device_id_type=MESH,
        ).wait()

    swaps[0].wait()
    scale = here[0][:, SIDE:] + partner[:, SIDE : 2 * SIDE] + REGULARIZER
    update(0, here[0][:, :SIDE] + partner[:, :SIDE], scale)
    send_all(spectra, values, 0, 2)
    swaps[1].wait()
    update(1, here[1] + partner[:, seconds], scale)
    send_all(spectra, values, 1, 4)
    templates = templates_ref[...]
    project = projection(templates)
    rebuild = lax.dot_general(
        templates, project, (((0,), (0,)), ((), ())), precision=HIGHEST, preferred_element_type=jnp.float32
    )
    solve = jnp.concatenate([rebuild, project], axis=0)
    for part in range(2):
        wait_all(2 + 2 * part)
        both = jnp.dot(solve, values[part], precision=HIGHEST, preferred_element_type=jnp.float32)
        answer[part] = both[:ENERGIES]
        coefficients[part] = both[ENERGIES:]
        for side in range(2):
            send_side(answer, fitted, part, 6 + 2 * part, side)
    for part in range(2):
        wait_all(6 + 2 * part)
        keep(part).wait()


SOURCES = 12


def hand_on(fitted, coefficients, fitted_out, coefficients_out, fitted_held, coefficients_held, sems):
    stages = [
        (fitted.at[part], fitted_held.at[part], fitted_out.at[part]) for part in range(2)
    ] + [(coefficients, coefficients_held, coefficients_out)]
    into = [pltpu.make_async_copy(a, b, sems.at[0, k]) for k, (a, b, c) in enumerate(stages)]
    onward = [pltpu.make_async_copy(b, c, sems.at[1, k]) for k, (a, b, c) in enumerate(stages)]
    for copy in into:
        copy.start()
    for first, second in zip(into, onward):
        first.wait()
        second.start()
    for copy in onward:
        copy.wait()


def local(
    sample_inphase,
    sample_quadrature,
    beam_inphase,
    beam_quadrature,
    recorded_diffraction,
    window_corners,
    filled_tallies,
    absorption_templates,
):
    vmem = pl.BlockSpec(memory_space=pltpu.VMEM)
    sources = (
        window_corners[0, 0].T,
        filled_tallies,
        sample_inphase,
        sample_quadrature,
        beam_inphase,
        beam_quadrature,
        recorded_diffraction,
        *[jnp.asarray(table) for table in dft_matrices()],
        absorption_templates,
    )
    rows = pltpu.VMEM((2, ENERGIES, SIDE), jnp.float32)
    fitted, coefficients = pl.pallas_call(
        step_kernel,
        out_shape=(
            jax.ShapeDtypeStruct((2, 1, ENERGIES, 1, SIDE), jnp.float32),
            jax.ShapeDtypeStruct((2, EDGES, SIDE), jnp.float32),
        ),
        in_specs=[pl.BlockSpec(memory_space=pl.ANY)] * SOURCES,
        out_specs=(pl.BlockSpec(memory_space=pl.ANY), vmem),
        scratch_shapes=[pltpu.SMEM(source.shape, source.dtype) for source in sources[:2]]
        + [pltpu.VMEM(source.shape, source.dtype) for source in sources[2:]]
        + [
            pltpu.VMEM((4 * SIDE, HALF), jnp.float32),
            pltpu.VMEM((HALF, 3 * SIDE), jnp.float32),
            pltpu.VMEM((HALF, 3 * SIDE), jnp.float32),
            rows,
            rows,
            rows,
            pltpu.VMEM((ENERGIES - 1, 1, SIDE), jnp.float32),
            pltpu.SemaphoreType.DMA((SOURCES,)),
            pltpu.SemaphoreType.DMA((14,)),
        ],
        compiler_params=pltpu.CompilerParams(
            collective_id=0, has_side_effects=True, vmem_limit_bytes=VMEM_BYTES
        ),
    )(*sources)
    whole = pl.BlockSpec(memory_space=pl.ANY)
    return pl.pallas_call(
        hand_on,
        out_shape=(
            jax.ShapeDtypeStruct(fitted.shape, jnp.float32),
            jax.ShapeDtypeStruct(coefficients.shape, jnp.float32),
        ),
        in_specs=[whole, whole],
        out_specs=(whole, whole),
        scratch_shapes=[
            pltpu.VMEM(fitted.shape, jnp.float32),
            pltpu.VMEM(coefficients.shape, jnp.float32),
            pltpu.SemaphoreType.DMA((2, 3)),
        ],
        compiler_params=pltpu.CompilerParams(vmem_limit_bytes=VMEM_BYTES),
    )(fitted, coefficients)


def solution(mesh):
    in_specs = (
        P("ea", None, None),
        P("ea", None, None),
        P("ea", None, None, None),
        P("ea", None, None, None),
        P("ea", "ta", None, None, None),
        P("ea", "ta", None, None),
        P("ea", "ta"),
        P(),
    )
    out_specs = (P(None, "ea", None, "ta", None), P(None, None, ("ea", "ta")))
    return jax.shard_map(local, mesh=mesh, in_specs=in_specs, out_specs=out_specs, check_vma=False)
```

```python
import functools

import jax
import jax.numpy as jnp
import numpy as np
from jax import lax
from jax.experimental import pallas as pl
from jax.experimental.pallas import tpu as pltpu
from jax.sharding import PartitionSpec as P

MESH = pl.DeviceIdType.MESH
HIGHEST = lax.Precision.HIGHEST
FLOOR_POWER = 0.5
REGULARIZER = 1.0
ENERGIES = 128
EDGES = 16
SIDE = 256
HALF = 128
WIDTH = 32
MODES = 3
SLOTS = 16
PER_GROUP = 4
GROUPS = SLOTS // PER_GROUP
BAND = MODES * WIDTH
LANES = PER_GROUP * WIDTH
VMEM_BYTES = 54 * 1024 * 1024


def split_table(table):
    high = table.astype(jnp.bfloat16)
    low = (table - high.astype(np.float32)).astype(jnp.bfloat16)
    return np.stack([high, low])


def dft_matrices():
    index = np.arange(WIDTH)
    angles = 2.0 * np.pi / WIDTH * (index[:, None] * index[None, :] % WIDTH)
    re, im = np.cos(angles) / np.sqrt(WIDTH), -np.sin(angles) / np.sqrt(WIDTH)
    tables = []
    for sign in (1.0, -1.0):
        b_re, b_im = (np.kron(np.eye(PER_GROUP), part) for part in (re, sign * im))
        l_re, l_im = (np.kron(np.eye(MODES), part) for part in (re, sign * im))
        right = np.block([[b_re, b_im], [-b_im, b_re]]).astype(np.float32)
        left = np.block([[l_re, -l_im], [l_im, l_re]]).astype(np.float32)
        tables += [split_table(right), split_table(left)]
    return tables


def halves(value):
    high = value.astype(jnp.bfloat16)
    return high, (value - high.astype(jnp.float32)).astype(jnp.bfloat16)


def product(a, b):
    dot = functools.partial(jnp.dot, preferred_element_type=jnp.float32)
    return dot(a[0], b[0]) + (dot(a[0], b[1]) + dot(a[1], b[0]))


def slot_terms(corners, tally, objects, p_re, p_im, intensity, right_f, left_f, right_b, left_b):
    probe_re = [jnp.concatenate([p_re[0, m]] * PER_GROUP, axis=1) for m in range(MODES)]
    probe_im = [jnp.concatenate([p_im[0, m]] * PER_GROUP, axis=1) for m in range(MODES)]
    light = sum(a * a + b * b for a, b in zip(probe_re, probe_im))
    lane = lax.broadcasted_iota(jnp.int32, (WIDTH, LANES), 1)

    bands = []
    for g in range(GROUPS):
        patch = [jnp.zeros((WIDTH, LANES), jnp.float32)] * 2
        for j in range(PER_GROUP):
            s = g * PER_GROUP + j
            row, column = corners[0, s], corners[1, s]
            shift = lax.rem(WIDTH * j + SIDE - column, HALF)
            for part in range(2):
                left, right = (objects[pl.ds(4 * row + 2 * part + half, WIDTH, stride=4), :] for half in range(2))
                rolled = pltpu.roll(jnp.where(lane >= column, left, right), shift, 1)
                patch[part] = jnp.where(lane // WIDTH == j, rolled, patch[part])
        exits_re = [a * patch[0] - b * patch[1] for a, b in zip(probe_re, probe_im)]
        exits_im = [a * patch[1] + b * patch[0] for a, b in zip(probe_re, probe_im)]
        bands.append(
            jnp.concatenate(
                [jnp.concatenate(exits_re, axis=0), jnp.concatenate(exits_im, axis=0)], axis=1
            )
        )
    wide = product(halves(jnp.concatenate(bands, axis=0)), (right_f[0], right_f[1]))
    tall = jnp.concatenate(
        [
            jnp.concatenate([wide[g * BAND : (g + 1) * BAND, h * LANES : (h + 1) * LANES] for g in range(GROUPS)], axis=1)
            for h in range(2)
        ],
        axis=0,
    )
    far = product((left_f[0], left_f[1]), halves(tall))
    power = sum(
        far[k * WIDTH : (k + 1) * WIDTH] * far[k * WIDTH : (k + 1) * WIDTH] for k in range(2 * MODES)
    )
    measured = jnp.concatenate([intensity[0, 0, s] for s in range(SLOTS)], axis=1)
    used = lax.broadcasted_iota(jnp.int32, (WIDTH, GROUPS * LANES), 1) // WIDTH < tally
    factor = jnp.where(used, 1.0 - jnp.sqrt(measured) / jnp.sqrt(jnp.maximum(power, FLOOR_POWER)), 0.0)
    corrected = far * jnp.concatenate([factor] * (2 * MODES), axis=0)
    tall = product((left_b[0], left_b[1]), halves(corrected))
    wide = jnp.concatenate(
        [
            jnp.concatenate([tall[h * BAND : (h + 1) * BAND, g * LANES : (g + 1) * LANES] for h in range(2)], axis=1)
            for g in range(GROUPS)
        ],
        axis=0,
    )
    back = product(halves(wide), (right_b[0], right_b[1]))
    placed = []
    for g in range(GROUPS):
        term_re, term_im = jnp.zeros((2, WIDTH, LANES), jnp.float32)
        for m in range(MODES):
            rows = slice(g * BAND + m * WIDTH, g * BAND + (m + 1) * WIDTH)
            b_re, b_im = back[rows, :LANES], back[rows, LANES:]
            term_re += probe_re[m] * b_re + probe_im[m] * b_im
            term_im += probe_re[m] * b_im - probe_im[m] * b_re
        for j in range(PER_GROUP):
            s = g * PER_GROUP + j
            column = corners[1, s]
            shift = lax.rem(column + HALF - WIDTH * j, HALF)
            weight = jnp.where(s < tally, 1.0, 0.0)
            parts = []
            for term in (term_re, light * weight, term_im):
                alone = pltpu.roll(jnp.where(lane // WIDTH == j, term, 0.0), shift, 1)
                parts += [jnp.where(lane >= column, alone, 0.0), jnp.where(lane < column, alone, 0.0)]
            placed.append(jnp.concatenate(parts, axis=1))
    return jnp.concatenate(placed, axis=0)


def row_choice(corners, parity):
    lane = lax.broadcasted_iota(jnp.int32, (HALF, LANES), 1)
    row = 2 * lax.broadcasted_iota(jnp.int32, (HALF, LANES), 0) + parity
    choices = []
    for g in range(GROUPS):
        first = jnp.zeros((HALF, LANES), jnp.int32)
        for j in range(PER_GROUP):
            first = jnp.where(lane // WIDTH == j, corners[0, g * PER_GROUP + j] - WIDTH * j, first)
        choices.append(jnp.where(row == first + lane, 1.0, 0.0).astype(jnp.bfloat16))
    return jnp.concatenate(choices, axis=1)


def projection(templates):
    gram = lax.dot_general(
        templates, templates, (((1,), (1,)), ((), ())), precision=HIGHEST, preferred_element_type=jnp.float32
    )
    table = jnp.concatenate(
        [gram, jnp.zeros((EDGES, ENERGIES - EDGES), jnp.float32), templates], axis=1
    )
    which = lax.broadcasted_iota(jnp.int32, table.shape, 0)
    for k in range(EDGES):
        pivot = table[k : k + 1, :] / table[k : k + 1, k : k + 1]
        table = jnp.where(which == k, pivot, table - table[:, k : k + 1] * pivot)
    return table[:, ENERGIES:]


def step_kernel(*refs):
    sources, (fitted, coefficients), (
        corners,
        tallies,
        o_re,
        o_im,
        p_re,
        p_im,
        intensity,
        right_f,
        left_f,
        right_b,
        left_b,
        templates_ref,
        objects,
        away,
        partner,
        spectra,
        values,
        answer,
        arrivals,
        local_sems,
        sems,
    ) = refs[:SOURCES], refs[SOURCES : SOURCES + 2], refs[SOURCES + 2 :]
    me, core = lax.axis_index("ea"), lax.axis_index("ta")
    copies = [
        pltpu.make_async_copy(source, target, local_sems.at[k])
        for k, (source, target) in enumerate(
            zip(
                sources,
                (corners, tallies, o_re, o_im, p_re, p_im, intensity, right_f, left_f, right_b, left_b, templates_ref),
            )
        )
    ]
    for copy in copies:
        copy.start()
    barrier = pltpu.get_barrier_semaphore()

    def peer_of(step):
        return lax.rem(me + 1 + step, ENERGIES)

    def greet(step, carry):
        pl.semaphore_signal(barrier, inc=1, device_id={"ea": peer_of(step)}, device_id_type=MESH)
        return carry

    pl.semaphore_signal(barrier, inc=1, device_id={"ta": 1 - core}, device_id_type=MESH)
    lax.fori_loop(0, ENERGIES - 1, greet, 0, unroll=8)
    for copy in copies:
        copy.wait()
    for part, source in enumerate((o_re, o_im)):
        for half in range(2):
            lanes = slice(half * HALF, (half + 1) * HALF)
            objects[pl.ds(2 * part + half, SIDE, stride=4), :] = source[0, :, lanes]
    placed = halves(
        slot_terms(corners, tallies[0, 0], objects, p_re, p_im, intensity, right_f, left_f, right_b, left_b)
    )

    def summed(choice, columns):
        dot = functools.partial(jnp.dot, preferred_element_type=jnp.float32)
        return dot(choice, placed[0][:, columns]) + dot(choice, placed[1][:, columns])

    def swap(lanes, first):
        return pltpu.make_async_remote_copy(
            src_ref=away.at[:, lanes],
            dst_ref=partner.at[:, lanes],
            send_sem=sems.at[first],
            recv_sem=sems.at[first + 1],
            device_id={"ta": 1 - core},
            device_id_type=MESH,
        )

    choice = row_choice(corners, 1 - core)
    firsts, seconds = slice(0, 2 * SIDE), slice(2 * SIDE, 3 * SIDE)
    swaps = [swap(pl.ds(0, 2 * SIDE), 0), swap(pl.ds(2 * SIDE, SIDE), 12)]
    away[:, firsts] = summed(choice, firsts)
    pl.semaphore_wait(barrier, ENERGIES)
    swaps[0].start()
    away[:, seconds] = summed(choice, seconds)
    swaps[1].start()
    choice = row_choice(corners, core)
    here = [summed(choice, firsts), summed(choice, seconds)]

    def update(part, total, scale):
        own = jnp.concatenate(
            [objects[pl.ds(4 * core + 2 * part + half, HALF, stride=8), :] for half in range(2)], axis=1
        )
        spectra[part] = own - total / scale

    x, y, depth = lax.rem(me, 4), me // 32, lax.rem(me // 4, 8)
    place = (y * 4 + lax.rem(depth, 4)) * 4 + x

    def landing(target, part):
        return target.at[part, pl.ds(me, 1)] if target is values else target.at[part, 0, me]

    def send_one(source, target, part, first, peer):
        pltpu.make_async_remote_copy(
            src_ref=source.at[part, pl.ds(peer, 1)],
            dst_ref=landing(target, part),
            send_sem=sems.at[first],
            recv_sem=sems.at[first + 1],
            device_id={"ea": peer},
            device_id_type=MESH,
        ).start()

    def send_all(source, target, part, first):
        def send(step, carry):
            send_one(source, target, part, first, peer_of(step))
            return carry

        lax.fori_loop(0, ENERGIES - 1, send, 0, unroll=8)
        target[part, pl.ds(me, 1), :] = source[part, pl.ds(me, 1), :]

    def keep(part):
        return pltpu.make_async_copy(answer.at[part, pl.ds(me, 1)], fitted.at[part, 0, me], sems.at[10 + part])

    def send_side(source, target, part, first, side):
        def send(step, carry):
            spot = lax.rem(place + step, 64)
            peer = (spot // 16) * 32 + side * 16 + lax.rem(spot, 16)
            send_one(source, target, part, first, peer)
            return carry

        if side == 0:
            across = (y * 8 + lax.rem(depth + 4, 8)) * 4 + x
            send_one(source, target, part, first, across)
            keep(part).start()
        lax.fori_loop(1, 64, send, 0, unroll=9)

    def wait_all(first):
        pltpu.make_async_remote_copy(
            src_ref=arrivals,
            dst_ref=arrivals,
            send_sem=sems.at[first],
            recv_sem=sems.at[first + 1],
            device_id={"ea": peer_of(0)},
            device_id_type=MESH,
        ).wait()

    swaps[0].wait()
    scale = here[0][:, SIDE:] + partner[:, SIDE : 2 * SIDE] + REGULARIZER
    update(0, here[0][:, :SIDE] + partner[:, :SIDE], scale)
    send_all(spectra, values, 0, 2)
    swaps[1].wait()
    update(1, here[1] + partner[:, seconds], scale)
    send_all(spectra, values, 1, 4)
    templates = templates_ref[...]
    project = projection(templates)
    rebuild = halves(
        lax.dot_general(
            templates, project, (((0,), (0,)), ((), ())), precision=HIGHEST, preferred_element_type=jnp.float32
        )
    )
    for part in range(2):
        wait_all(2 + 2 * part)
        answer[part] = product(rebuild, halves(values[part]))
        for side in range(2):
            send_side(answer, fitted, part, 6 + 2 * part, side)
        coefficients[part] = jnp.dot(
            project, values[part], precision=HIGHEST, preferred_element_type=jnp.float32
        )
    for part in range(2):
        wait_all(6 + 2 * part)
        keep(part).wait()


SOURCES = 12


def hand_on(fitted, coefficients, fitted_out, coefficients_out, fitted_held, coefficients_held, sems):
    stages = [
        (fitted.at[part], fitted_held.at[part], fitted_out.at[part]) for part in range(2)
    ] + [(coefficients, coefficients_held, coefficients_out)]
    into = [pltpu.make_async_copy(a, b, sems.at[0, k]) for k, (a, b, c) in enumerate(stages)]
    onward = [pltpu.make_async_copy(b, c, sems.at[1, k]) for k, (a, b, c) in enumerate(stages)]
    for copy in into:
        copy.start()
    for first, second in zip(into, onward):
        first.wait()
        second.start()
    for copy in onward:
        copy.wait()


def local(
    sample_inphase,
    sample_quadrature,
    beam_inphase,
    beam_quadrature,
    recorded_diffraction,
    window_corners,
    filled_tallies,
    absorption_templates,
):
    vmem = pl.BlockSpec(memory_space=pltpu.VMEM)
    sources = (
        window_corners[0, 0].T,
        filled_tallies,
        sample_inphase,
        sample_quadrature,
        beam_inphase,
        beam_quadrature,
        recorded_diffraction,
        *[jnp.asarray(table) for table in dft_matrices()],
        absorption_templates,
    )
    rows = pltpu.VMEM((2, ENERGIES, SIDE), jnp.float32)
    fitted, coefficients = pl.pallas_call(
        step_kernel,
        out_shape=(
            jax.ShapeDtypeStruct((2, 1, ENERGIES, 1, SIDE), jnp.float32),
            jax.ShapeDtypeStruct((2, EDGES, SIDE), jnp.float32),
        ),
        in_specs=[pl.BlockSpec(memory_space=pl.ANY)] * SOURCES,
        out_specs=(pl.BlockSpec(memory_space=pl.ANY), vmem),
        scratch_shapes=[pltpu.SMEM(source.shape, source.dtype) for source in sources[:2]]
        + [pltpu.VMEM(source.shape, source.dtype) for source in sources[2:]]
        + [
            pltpu.VMEM((4 * SIDE, HALF), jnp.float32),
            pltpu.VMEM((HALF, 3 * SIDE), jnp.float32),
            pltpu.VMEM((HALF, 3 * SIDE), jnp.float32),
            rows,
            rows,
            rows,
            pltpu.VMEM((ENERGIES - 1, 1, SIDE), jnp.float32),
            pltpu.SemaphoreType.DMA((SOURCES,)),
            pltpu.SemaphoreType.DMA((14,)),
        ],
        compiler_params=pltpu.CompilerParams(
            collective_id=0, has_side_effects=True, vmem_limit_bytes=VMEM_BYTES
        ),
    )(*sources)
    whole = pl.BlockSpec(memory_space=pl.ANY)
    return pl.pallas_call(
        hand_on,
        out_shape=(
            jax.ShapeDtypeStruct(fitted.shape, jnp.float32),
            jax.ShapeDtypeStruct(coefficients.shape, jnp.float32),
        ),
        in_specs=[whole, whole],
        out_specs=(whole, whole),
        scratch_shapes=[
            pltpu.VMEM(fitted.shape, jnp.float32),
            pltpu.VMEM(coefficients.shape, jnp.float32),
            pltpu.SemaphoreType.DMA((2, 3)),
        ],
        compiler_params=pltpu.CompilerParams(vmem_limit_bytes=VMEM_BYTES),
    )(fitted, coefficients)


def solution(mesh):
    in_specs = (
        P("ea", None, None),
        P("ea", None, None),
        P("ea", None, None, None),
        P("ea", None, None, None),
        P("ea", "ta", None, None, None),
        P("ea", "ta", None, None),
        P("ea", "ta"),
        P(),
    )
    out_specs = (P(None, "ea", None, "ta", None), P(None, None, ("ea", "ta")))
    return jax.shard_map(local, mesh=mesh, in_specs=in_specs, out_specs=out_specs, check_vma=False)
```

```python
import functools

import jax
import jax.numpy as jnp
import numpy as np
from jax import lax
from jax.experimental import pallas as pl
from jax.experimental.pallas import tpu as pltpu
from jax.sharding import PartitionSpec as P

MESH = pl.DeviceIdType.MESH
HIGHEST = lax.Precision.HIGHEST
FLOOR_POWER = 0.5
REGULARIZER = 1.0
ENERGIES = 128
EDGES = 16
SIDE = 256
HALF = 128
WIDTH = 32
MODES = 3
SLOTS = 16
PER_GROUP = 4
GROUPS = SLOTS // PER_GROUP
BAND = MODES * WIDTH
LANES = PER_GROUP * WIDTH
VMEM_BYTES = 54 * 1024 * 1024


def split_table(table):
    high = table.astype(jnp.bfloat16)
    low = (table - high.astype(np.float32)).astype(jnp.bfloat16)
    return np.stack([high, low])


def dft_matrices():
    index = np.arange(WIDTH)
    angles = 2.0 * np.pi / WIDTH * (index[:, None] * index[None, :] % WIDTH)
    re, im = np.cos(angles) / np.sqrt(WIDTH), -np.sin(angles) / np.sqrt(WIDTH)
    tables = []
    for sign in (1.0, -1.0):
        b_re, b_im = (np.kron(np.eye(PER_GROUP), part) for part in (re, sign * im))
        l_re, l_im = (np.kron(np.eye(MODES), part) for part in (re, sign * im))
        right = np.block([[b_re, b_im], [-b_im, b_re]]).astype(np.float32)
        left = np.block([[l_re, -l_im], [l_im, l_re]]).astype(np.float32)
        tables += [split_table(right), split_table(left)]
    return tables


def halves(value):
    high = value.astype(jnp.bfloat16)
    return high, (value - high.astype(jnp.float32)).astype(jnp.bfloat16)


def product(a, b):
    dot = functools.partial(jnp.dot, preferred_element_type=jnp.float32)
    return dot(a[0], b[0]) + (dot(a[0], b[1]) + dot(a[1], b[0]))


def slot_terms(corners, tally, objects, p_re, p_im, intensity, right_f, left_f, right_b, left_b):
    probe_re = [jnp.concatenate([p_re[0, m]] * PER_GROUP, axis=1) for m in range(MODES)]
    probe_im = [jnp.concatenate([p_im[0, m]] * PER_GROUP, axis=1) for m in range(MODES)]
    light = sum(a * a + b * b for a, b in zip(probe_re, probe_im))
    lane = lax.broadcasted_iota(jnp.int32, (WIDTH, LANES), 1)

    bands = []
    for g in range(GROUPS):
        patch = [jnp.zeros((WIDTH, LANES), jnp.float32)] * 2
        for j in range(PER_GROUP):
            s = g * PER_GROUP + j
            row, column = corners[0, s], corners[1, s]
            shift = lax.rem(WIDTH * j + SIDE - column, HALF)
            for part in range(2):
                left, right = (objects[pl.ds(4 * row + 2 * part + half, WIDTH, stride=4), :] for half in range(2))
                rolled = pltpu.roll(jnp.where(lane >= column, left, right), shift, 1)
                patch[part] = jnp.where(lane // WIDTH == j, rolled, patch[part])
        exits_re = [a * patch[0] - b * patch[1] for a, b in zip(probe_re, probe_im)]
        exits_im = [a * patch[1] + b * patch[0] for a, b in zip(probe_re, probe_im)]
        bands.append(
            jnp.concatenate(
                [jnp.concatenate(exits_re, axis=0), jnp.concatenate(exits_im, axis=0)], axis=1
            )
        )
    wide = product(halves(jnp.concatenate(bands, axis=0)), (right_f[0], right_f[1]))
    tall = jnp.concatenate(
        [
            jnp.concatenate([wide[g * BAND : (g + 1) * BAND, h * LANES : (h + 1) * LANES] for g in range(GROUPS)], axis=1)
            for h in range(2)
        ],
        axis=0,
    )
    far = product((left_f[0], left_f[1]), halves(tall))
    power = sum(
        far[k * WIDTH : (k + 1) * WIDTH] * far[k * WIDTH : (k + 1) * WIDTH] for k in range(2 * MODES)
    )
    measured = jnp.concatenate([intensity[0, 0, s] for s in range(SLOTS)], axis=1)
    used = lax.broadcasted_iota(jnp.int32, (WIDTH, GROUPS * LANES), 1) // WIDTH < tally
    factor = jnp.where(used, 1.0 - jnp.sqrt(measured) / jnp.sqrt(jnp.maximum(power, FLOOR_POWER)), 0.0)
    corrected = far * jnp.concatenate([factor] * (2 * MODES), axis=0)
    tall = product((left_b[0], left_b[1]), halves(corrected))
    wide = jnp.concatenate(
        [
            jnp.concatenate([tall[h * BAND : (h + 1) * BAND, g * LANES : (g + 1) * LANES] for h in range(2)], axis=1)
            for g in range(GROUPS)
        ],
        axis=0,
    )
    back = product(halves(wide), (right_b[0], right_b[1]))
    placed = []
    for g in range(GROUPS):
        term_re, term_im = jnp.zeros((2, WIDTH, LANES), jnp.float32)
        for m in range(MODES):
            rows = slice(g * BAND + m * WIDTH, g * BAND + (m + 1) * WIDTH)
            b_re, b_im = back[rows, :LANES], back[rows, LANES:]
            term_re += probe_re[m] * b_re + probe_im[m] * b_im
            term_im += probe_re[m] * b_im - probe_im[m] * b_re
        for j in range(PER_GROUP):
            s = g * PER_GROUP + j
            column = corners[1, s]
            shift = lax.rem(column + HALF - WIDTH * j, HALF)
            weight = jnp.where(s < tally, 1.0, 0.0)
            parts = []
            for term in (term_re, light * weight, term_im):
                alone = pltpu.roll(jnp.where(lane // WIDTH == j, term, 0.0), shift, 1)
                parts += [jnp.where(lane >= column, alone, 0.0), jnp.where(lane < column, alone, 0.0)]
            placed.append(jnp.concatenate(parts, axis=1))
    return jnp.concatenate(placed, axis=0)


def row_choice(corners, parity):
    lane = lax.broadcasted_iota(jnp.int32, (HALF, LANES), 1)
    row = 2 * lax.broadcasted_iota(jnp.int32, (HALF, LANES), 0) + parity
    choices = []
    for g in range(GROUPS):
        first = jnp.zeros((HALF, LANES), jnp.int32)
        for j in range(PER_GROUP):
            first = jnp.where(lane // WIDTH == j, corners[0, g * PER_GROUP + j] - WIDTH * j, first)
        choices.append(jnp.where(row == first + lane, 1.0, 0.0).astype(jnp.bfloat16))
    return jnp.concatenate(choices, axis=1)


def projection(templates):
    gram = lax.dot_general(
        templates, templates, (((1,), (1,)), ((), ())), precision=HIGHEST, preferred_element_type=jnp.float32
    )
    table = jnp.concatenate(
        [gram, jnp.zeros((EDGES, ENERGIES - EDGES), jnp.float32), templates], axis=1
    )
    which = lax.broadcasted_iota(jnp.int32, table.shape, 0)
    for k in range(EDGES):
        pivot = table[k : k + 1, :] / table[k : k + 1, k : k + 1]
        table = jnp.where(which == k, pivot, table - table[:, k : k + 1] * pivot)
    return table[:, ENERGIES:]


def step_kernel(*refs):
    sources, (fitted, coefficients), (
        corners,
        tallies,
        o_re,
        o_im,
        p_re,
        p_im,
        intensity,
        right_f,
        left_f,
        right_b,
        left_b,
        templates_ref,
        objects,
        away,
        partner,
        spectra,
        values,
        answer,
        arrivals,
        local_sems,
        sems,
    ) = refs[:SOURCES], refs[SOURCES : SOURCES + 2], refs[SOURCES + 2 :]
    me, core = lax.axis_index("ea"), lax.axis_index("ta")
    copies = [
        pltpu.make_async_copy(source, target, local_sems.at[k])
        for k, (source, target) in enumerate(
            zip(
                sources,
                (corners, tallies, o_re, o_im, p_re, p_im, intensity, right_f, left_f, right_b, left_b, templates_ref),
            )
        )
    ]
    for copy in copies:
        copy.start()
    barrier = pltpu.get_barrier_semaphore()

    def peer_of(step):
        return lax.rem(me + 1 + step, ENERGIES)

    def greet(step, carry):
        pl.semaphore_signal(barrier, inc=1, device_id={"ea": peer_of(step)}, device_id_type=MESH)
        return carry

    pl.semaphore_signal(barrier, inc=1, device_id={"ta": 1 - core}, device_id_type=MESH)
    lax.fori_loop(0, ENERGIES - 1, greet, 0, unroll=8)
    for copy in copies:
        copy.wait()
    for part, source in enumerate((o_re, o_im)):
        for half in range(2):
            lanes = slice(half * HALF, (half + 1) * HALF)
            objects[pl.ds(2 * part + half, SIDE, stride=4), :] = source[0, :, lanes]
    placed = halves(
        slot_terms(corners, tallies[0, 0], objects, p_re, p_im, intensity, right_f, left_f, right_b, left_b)
    )

    def summed(choice, columns):
        dot = functools.partial(jnp.dot, preferred_element_type=jnp.float32)
        return dot(choice, placed[0][:, columns]) + dot(choice, placed[1][:, columns])

    def swap(lanes, first):
        return pltpu.make_async_remote_copy(
            src_ref=away.at[:, lanes],
            dst_ref=partner.at[:, lanes],
            send_sem=sems.at[first],
            recv_sem=sems.at[first + 1],
            device_id={"ta": 1 - core},
            device_id_type=MESH,
        )

    choice = row_choice(corners, 1 - core)
    firsts, seconds = slice(0, 2 * SIDE), slice(2 * SIDE, 3 * SIDE)
    swaps = [swap(pl.ds(0, 2 * SIDE), 0), swap(pl.ds(2 * SIDE, SIDE), 12)]
    away[:, firsts] = summed(choice, firsts)
    pl.semaphore_wait(barrier, ENERGIES)
    swaps[0].start()
    away[:, seconds] = summed(choice, seconds)
    swaps[1].start()
    choice = row_choice(corners, core)
    here = [summed(choice, firsts), summed(choice, seconds)]

    def update(part, total, scale):
        own = jnp.concatenate(
            [objects[pl.ds(4 * core + 2 * part + half, HALF, stride=8), :] for half in range(2)], axis=1
        )
        spectra[part] = own - total / scale

    x, y, depth = lax.rem(me, 4), me // 32, lax.rem(me // 4, 8)
    place = (y * 4 + lax.rem(depth, 4)) * 4 + x

    def landing(target, part):
        return target.at[part, pl.ds(me, 1)] if target is values else target.at[part, 0, me]

    def send_one(source, target, part, first, peer):
        pltpu.make_async_remote_copy(
            src_ref=source.at[part, pl.ds(peer, 1)],
            dst_ref=landing(target, part),
            send_sem=sems.at[first],
            recv_sem=sems.at[first + 1],
            device_id={"ea": peer},
            device_id_type=MESH,
        ).start()

    def send_all(source, target, part, first):
        def send(step, carry):
            send_one(source, target, part, first, peer_of(step))
            return carry

        lax.fori_loop(0, ENERGIES - 1, send, 0, unroll=8)
        target[part, pl.ds(me, 1), :] = source[part, pl.ds(me, 1), :]

    def keep(part):
        return pltpu.make_async_copy(answer.at[part, pl.ds(me, 1)], fitted.at[part, 0, me], sems.at[10 + part])

    def send_side(source, target, part, first, side):
        def send(step, carry):
            spot = lax.rem(place + step, 64)
            peer = (spot // 16) * 32 + side * 16 + lax.rem(spot, 16)
            send_one(source, target, part, first, peer)
            return carry

        if side == 0:
            across = (y * 8 + lax.rem(depth + 4, 8)) * 4 + x
            send_one(source, target, part, first, across)
            keep(part).start()
        lax.fori_loop(1, 64, send, 0, unroll=9)

    def wait_all(first):
        pltpu.make_async_remote_copy(
            src_ref=arrivals,
            dst_ref=arrivals,
            send_sem=sems.at[first],
            recv_sem=sems.at[first + 1],
            device_id={"ea": peer_of(0)},
            device_id_type=MESH,
        ).wait()

    swaps[0].wait()
    scale = here[0][:, SIDE:] + partner[:, SIDE : 2 * SIDE] + REGULARIZER
    update(0, here[0][:, :SIDE] + partner[:, :SIDE], scale)
    send_all(spectra, values, 0, 2)
    swaps[1].wait()
    update(1, here[1] + partner[:, seconds], scale)
    send_all(spectra, values, 1, 4)
    templates = templates_ref[...]
    project = projection(templates)
    rebuild = lax.dot_general(
        templates, project, (((0,), (0,)), ((), ())), precision=HIGHEST, preferred_element_type=jnp.float32
    )
    solve = jnp.concatenate([rebuild, project], axis=0)
    for part in range(2):
        wait_all(2 + 2 * part)
        both = jnp.dot(solve, values[part], precision=HIGHEST, preferred_element_type=jnp.float32)
        answer[part] = both[:ENERGIES]
        coefficients[part] = both[ENERGIES:]
        for side in range(2):
            send_side(answer, fitted, part, 6 + 2 * part, side)
    for part in range(2):
        wait_all(6 + 2 * part)
        keep(part).wait()


SOURCES = 12


def hand_on(fitted, coefficients, fitted_out, coefficients_out, fitted_held, coefficients_held, sems):
    stages = [
        tuple(ref.at[part, :, pl.ds(first, 64)] for ref in (fitted, fitted_held, fitted_out))
        for part in range(2)
        for first in range(0, ENERGIES, 64)
    ] + [(coefficients, coefficients_held, coefficients_out)]
    into = [pltpu.make_async_copy(a, b, sems.at[0, k]) for k, (a, b, c) in enumerate(stages)]
    onward = [pltpu.make_async_copy(b, c, sems.at[1, k]) for k, (a, b, c) in enumerate(stages)]
    for copy in into:
        copy.start()
    for first, second in zip(into, onward):
        first.wait()
        second.start()
    for copy in onward:
        copy.wait()


def local(
    sample_inphase,
    sample_quadrature,
    beam_inphase,
    beam_quadrature,
    recorded_diffraction,
    window_corners,
    filled_tallies,
    absorption_templates,
):
    vmem = pl.BlockSpec(memory_space=pltpu.VMEM)
    sources = (
        window_corners[0, 0].T,
        filled_tallies,
        sample_inphase,
        sample_quadrature,
        beam_inphase,
        beam_quadrature,
        recorded_diffraction,
        *[jnp.asarray(table) for table in dft_matrices()],
        absorption_templates,
    )
    rows = pltpu.VMEM((2, ENERGIES, SIDE), jnp.float32)
    fitted, coefficients = pl.pallas_call(
        step_kernel,
        out_shape=(
            jax.ShapeDtypeStruct((2, 1, ENERGIES, 1, SIDE), jnp.float32),
            jax.ShapeDtypeStruct((2, EDGES, SIDE), jnp.float32),
        ),
        in_specs=[pl.BlockSpec(memory_space=pl.ANY)] * SOURCES,
        out_specs=(pl.BlockSpec(memory_space=pl.ANY), vmem),
        scratch_shapes=[pltpu.SMEM(source.shape, source.dtype) for source in sources[:2]]
        + [pltpu.VMEM(source.shape, source.dtype) for source in sources[2:]]
        + [
            pltpu.VMEM((4 * SIDE, HALF), jnp.float32),
            pltpu.VMEM((HALF, 3 * SIDE), jnp.float32),
            pltpu.VMEM((HALF, 3 * SIDE), jnp.float32),
            rows,
            rows,
            rows,
            pltpu.VMEM((ENERGIES - 1, 1, SIDE), jnp.float32),
            pltpu.SemaphoreType.DMA((SOURCES,)),
            pltpu.SemaphoreType.DMA((14,)),
        ],
        compiler_params=pltpu.CompilerParams(
            collective_id=0, has_side_effects=True, vmem_limit_bytes=VMEM_BYTES
        ),
    )(*sources)
    whole = pl.BlockSpec(memory_space=pl.ANY)
    return pl.pallas_call(
        hand_on,
        out_shape=(
            jax.ShapeDtypeStruct(fitted.shape, jnp.float32),
            jax.ShapeDtypeStruct(coefficients.shape, jnp.float32),
        ),
        in_specs=[whole, whole],
        out_specs=(whole, whole),
        scratch_shapes=[
            pltpu.VMEM(fitted.shape, jnp.float32),
            pltpu.VMEM(coefficients.shape, jnp.float32),
            pltpu.SemaphoreType.DMA((2, 5)),
        ],
        compiler_params=pltpu.CompilerParams(vmem_limit_bytes=VMEM_BYTES),
    )(fitted, coefficients)


def solution(mesh):
    in_specs = (
        P("ea", None, None),
        P("ea", None, None),
        P("ea", None, None, None),
        P("ea", None, None, None),
        P("ea", "ta", None, None, None),
        P("ea", "ta", None, None),
        P("ea", "ta"),
        P(),
    )
    out_specs = (P(None, "ea", None, "ta", None), P(None, None, ("ea", "ta")))
    return jax.shard_map(local, mesh=mesh, in_specs=in_specs, out_specs=out_specs, check_vma=False)
```
